512 devices in a mesh: ctx: 64 (over y, z), exp: 8 (over x, core).
Axes of the slice: x: 4, y: 4, z: 16, core: 2. Of those that a mesh axis runs over, the one named last changes fastest.
Arguments:
- x_resid: bfloat16 [512, 6144], P('exp', 'ctx'), may hold values from -16 to 16
- queries: bfloat16 [512, 6144], P('ctx', 'exp'), may hold values from -5 to 5
- keys: bfloat16 [32768, 1024], P('ctx', 'exp'), may hold values from -4 to 4
- values: bfloat16 [32768, 1024], P('ctx', 'exp'), may hold values from -4 to 4
- pattern: int32 [4, 6], replicated, may hold values from 0 to 254, as said below
- global_blocks: int32 [2], replicated, may hold values from 0 to 248, as said below
- out_weight: bfloat16 [6144, 6144], P('exp', 'ctx'), may hold values from -0.875 to 0.875
- norm_gain: float32 [6144], P('ctx'), may hold values from 0.1 to 1.9
- router: bfloat16 [6144, 8], P('ctx'), may hold values from -0.078125 to 0.078125
- expert_ids: int32 [512, 2], P('exp'), may hold values from 0 to 7, as said below
- expert_slots: int32 [512, 2], P('exp'), may hold values from 0 to 19, as said below
- w_gate: bfloat16 [8, 6144, 8192], P('exp', None, 'ctx'), may hold values from -0.078125 to 0.078125
- w_up: bfloat16 [8, 6144, 8192], P('exp', None, 'ctx'), may hold values from -0.078125 to 0.078125
- w_down: bfloat16 [8, 8192, 6144], P('exp', None, 'ctx'), may hold values from -0.0625 to 0.0625
Outputs:
- layer_out: bfloat16 [512, 6144], P('exp', 'ctx')
The draws below stay inside these ranges and needn't reach their ends.
Inputs may be any that keep to these rules, and one draw needn't show every extreme that they name: `pattern`: each row lists 3 + 3 different key blocks, none of them a global block. `global_blocks`: 2 different key blocks. `expert_ids`: each token names two different experts; among the tokens of one index of exp (aligned blocks of 64 rows) every expert is named at most 20 times, and one expert, the same in every block, exactly 20 times. `expert_slots`: within one aligned block of 64 rows, the choices that name the same expert have different slots.
All inputs are finite; a program needn't handle non-finite values.
Results may differ from the reference program's by a relative error of at most 0.01.
Values may be sent and summed in bfloat16 or wider, within the bound.
No kernel may reach another device: no remote copies, remote signals or barrier semaphores. Data moves between devices by JAX's collectives and lax.ppermute only.
A program may use at most 64 MiB of HBM per device.

```python
import jax
import jax.numpy as jnp
from jax import lax

D = 6144
H = 48
KVH = 8
HD = 128
E = 8
FFW = 8192
BLK = 128
NWIN = 3
NRAND = 3
NGLOB = 2
TOK_EXP = 64
TOK = 512
CACHE = 32768
QB = 4
KB = 256
CAP = 20
N_EXP = 8


def block_plan(key):
    base = jax.random.fold_in(key, 101)
    pool = KB - QB - NWIN
    order = jax.random.permutation(jax.random.fold_in(base, 1), pool - 1).astype(jnp.int32)
    last_block = jnp.full((1,), pool - 1, dtype=jnp.int32)
    anchors = jnp.concatenate([last_block, order[:NGLOB - 1]]).astype(jnp.int32)
    remaining = order[NGLOB - 1:]

    def one_row(index):
        picks = jax.random.permutation(jax.random.fold_in(base, index + 2), pool - NGLOB)[:NRAND]
        window = KB - QB + index - NWIN + jnp.arange(NWIN, dtype=jnp.int32)
        return jnp.concatenate([window.astype(jnp.int32), remaining[picks].astype(jnp.int32)])
    rows = jax.vmap(one_row)(jnp.arange(QB, dtype=jnp.int32))
    return (anchors, rows)


def route_plan(key):
    base = jax.random.fold_in(key, 707)
    hottest = jax.random.randint(jax.random.fold_in(base, 1), (), 0, E).astype(jnp.int32)
    cycle = jax.random.permutation(jax.random.fold_in(base, 2), E - 1).astype(jnp.int32)

    def one_block(index):
        inner = jax.random.fold_in(base, index + 3)
        order = jax.random.permutation(jax.random.fold_in(inner, 1), TOK_EXP).astype(jnp.int32)
        offset = jax.random.randint(jax.random.fold_in(inner, 2), (), 0, E - 1).astype(jnp.int32)
        rank = jnp.argsort(order, stable=True).astype(jnp.int32)
        leading = rank < CAP
        first_step = jnp.where(leading, rank, 2 * rank - CAP)
        second_step = jnp.where(leading, rank, 2 * rank - CAP + 1)

        def assign(step):
            turn = step + offset
            member = cycle[turn % (E - 1)]
            return (member + (member >= hottest).astype(jnp.int32), turn // (E - 1))
        first_expert, first_slot = assign(first_step)
        second_expert, second_slot = assign(second_step)
        first_expert = jnp.where(leading, hottest, first_expert)
        first_slot = jnp.where(leading, rank, first_slot)
        chosen = jnp.stack([first_expert, second_expert], axis=1).astype(jnp.int32)
        placed = jnp.stack([first_slot, second_slot], axis=1).astype(jnp.int32)
        return (chosen, placed)
    chosen, placed = jax.vmap(one_block)(jnp.arange(TOK // TOK_EXP, dtype=jnp.int32))
    return (chosen.reshape(TOK, 2), placed.reshape(TOK, 2))


def draw_x_resid(key, part):
    base = jax.random.fold_in(key, 606)
    columns = jnp.exp(jnp.log(3.0) * jnp.arange(D, dtype=jnp.float32) / D)
    field = jnp.clip(jax.random.normal(base, (TOK, D), jnp.float32), -4.0, 4.0)
    return (0.3 * field * columns[None, :]).astype(jnp.bfloat16)


def draw_queries(key, part):
    base = jax.random.fold_in(key, 505)
    field = jnp.clip(jax.random.normal(base, (TOK, H * HD), jnp.float32), -4.0, 4.0)
    return field.astype(jnp.bfloat16)


def draw_keys(key, part):
    base = jax.random.fold_in(key, 404)
    field = jnp.clip(jax.random.normal(base, (CACHE, KVH * HD), jnp.float32), -4.0, 4.0)
    return field.astype(jnp.bfloat16)


def draw_pattern(key, part):
    anchors, listed = block_plan(key)
    return listed


def draw_global_blocks(key, part):
    anchors, listed = block_plan(key)
    return anchors


def draw_expert_ids(key, part):
    chosen, placed = route_plan(key)
    return chosen


def draw_expert_slots(key, part):
    chosen, placed = route_plan(key)
    return placed


def levels(key, extent, cuts, smallest, high):
    level = 1.0
    for dim, blocks in cuts:
        steps = jax.random.uniform(jax.random.fold_in(jax.random.fold_in(key, 6), dim), (blocks,), jnp.float32, smallest / len(cuts), high / len(cuts))
        level = level * jnp.repeat(jnp.exp(steps), extent[dim] // blocks).reshape((-1,) + (1,) * (len(extent) - 1 - dim))
    return level


def noise(stream_key, shape, scale, most, shards=(), kind=jnp.bfloat16):
    loudness = levels(stream_key, shape, shards, -0.22, 0.18) if shards else 1.0
    entries = jax.random.normal(stream_key, shape, jnp.float32) * scale * loudness
    return jnp.minimum(jnp.maximum(entries, -most), most).astype(kind)


def setup_inputs(seed: int = 0) -> dict:
    arg_keys = jax.random.split(jax.random.key(seed), 15)
    x_resid = draw_x_resid(jax.random.fold_in(arg_keys[14], 71), 0)
    queries = draw_queries(jax.random.fold_in(arg_keys[14], 71), 0)
    keys = draw_keys(jax.random.fold_in(arg_keys[14], 71), 0)
    values = noise(arg_keys[3], (CACHE, KVH * HD), 1.0, 4.0, ((0, 64), (1, 8)))
    pattern = draw_pattern(jax.random.fold_in(arg_keys[14], 71), 0)
    global_blocks = draw_global_blocks(jax.random.fold_in(arg_keys[14], 71), 0)
    out_weight = noise(arg_keys[6], (H * HD, D), 0.15, 0.875, ((0, 8), (1, 64)))
    norm_gain = jnp.clip(1.0 + 0.18 * jax.random.normal(arg_keys[7], (D,), jnp.float32), 0.1, 1.9)
    router = noise(arg_keys[8], (D, E), D ** -0.5, 0.078125, ((0, 64),))
    expert_ids = draw_expert_ids(jax.random.fold_in(arg_keys[14], 71), 0)
    expert_slots = draw_expert_slots(jax.random.fold_in(arg_keys[14], 71), 0)
    w_gate = noise(arg_keys[11], (E, D, FFW), D ** -0.5, 0.078125, ((0, 8), (2, 64)))
    w_up = noise(arg_keys[12], (E, D, FFW), D ** -0.5, 0.078125, ((0, 8), (2, 64)))
    w_down = noise(arg_keys[13], (E, FFW, D), FFW ** -0.5, 0.0625, ((0, 8), (2, 64)))
    return {"x_resid": x_resid, "queries": queries, "keys": keys, "values": values, "pattern": pattern, "global_blocks": global_blocks, "out_weight": out_weight, "norm_gain": norm_gain, "router": router, "expert_ids": expert_ids, "expert_slots": expert_slots, "w_gate": w_gate, "w_up": w_up, "w_down": w_down}


eps = 1e-05

def reference(x_resid, queries, keys, values, pattern, global_blocks, out_weight, norm_gain, router, expert_ids, expert_slots, w_gate, w_up, w_down):
    group = H // KVH
    key_blocks = keys.reshape(KB, BLK, KVH, HD)
    value_blocks = values.reshape(KB, BLK, KVH, HD)
    query_blocks = queries.reshape(QB, BLK, KVH, group, HD)

    def attend(inputs):
        query_block, listed = inputs
        chosen = jnp.concatenate([listed, global_blocks]).astype(jnp.int32)
        key_set = key_blocks[chosen].reshape(-1, KVH, HD).astype(jnp.float32)
        value_set = value_blocks[chosen].reshape(-1, KVH, HD).astype(jnp.float32)
        scores = jnp.einsum('tkgd,pkd->tkgp', query_block.astype(jnp.float32), key_set, precision=lax.Precision.HIGHEST) * HD ** (-0.5)
        peak = lax.optimization_barrier(jnp.max(scores, axis=-1, keepdims=True))
        probs = jnp.exp(scores - peak).astype(jnp.bfloat16)
        numerator = jnp.einsum('tkgp,pkd->tkgd', probs.astype(jnp.float32), value_set, precision=lax.Precision.HIGHEST)
        denominator = lax.optimization_barrier(jnp.sum(probs.astype(jnp.float32), axis=-1))
        return (numerator / denominator[..., None]).astype(jnp.bfloat16)
    attention = lax.map(attend, (query_blocks, pattern)).reshape(TOK, H * HD)
    residual = x_resid.astype(jnp.float32) + jnp.dot(attention, out_weight, preferred_element_type=jnp.float32)
    inverse = lax.rsqrt(lax.optimization_barrier(jnp.sum(residual * residual, axis=1)) / D + eps)
    scaled = residual * norm_gain
    normed = (scaled * inverse[:, None]).astype(jnp.bfloat16)
    logits = inverse[:, None] * jnp.dot(scaled, router.astype(jnp.float32), precision=lax.Precision.HIGHEST)
    onehot = expert_ids[:, :, None] == jnp.arange(E, dtype=jnp.int32)[None, None, :]
    chosen_logits = lax.optimization_barrier(jnp.sum(jnp.where(onehot, logits[:, None, :], 0.0), axis=-1))
    gate_weights = jax.nn.sigmoid(chosen_logits - chosen_logits[:, ::-1])
    source = jnp.arange(TOK, dtype=jnp.int32) // TOK_EXP
    flat_slots = (expert_ids * CAP + expert_slots).astype(jnp.int32)
    buffers = jnp.zeros((N_EXP, E * CAP, D), jnp.bfloat16)
    buffers = buffers.at[source[:, None], flat_slots].set(jnp.broadcast_to(normed[:, None, :], (TOK, 2, D)))
    per_expert = buffers.reshape(N_EXP, E, CAP, D).transpose(1, 0, 2, 3).reshape(E, N_EXP * CAP, D)

    def expert(inputs):
        rows, gate_matrix, lift_matrix, down_matrix = inputs
        expert_gate = jnp.dot(rows, gate_matrix, preferred_element_type=jnp.float32)
        expert_lift = jnp.dot(rows, lift_matrix, preferred_element_type=jnp.float32)
        hidden = (jax.nn.silu(expert_gate) * expert_lift).astype(jnp.bfloat16)
        return jnp.dot(hidden, down_matrix, preferred_element_type=jnp.float32).astype(jnp.bfloat16)
    expert_out = lax.map(expert, (per_expert, w_gate, w_up, w_down)).reshape(E, N_EXP, CAP, D)
    picked = expert_out[expert_ids, source[:, None], expert_slots].astype(jnp.float32)
    mixture = lax.optimization_barrier(jnp.sum(gate_weights[:, :, None] * picked, axis=1))
    return (residual + mixture).astype(jnp.bfloat16)
```

```python
import jax
import jax.numpy as jnp
from jax import lax
from jax.experimental import pallas as pl
from jax.experimental.pallas import tpu as pltpu
from jax.sharding import Mesh, PartitionSpec as P

D = 6144
HD = 128
BLK = 128
CAP = 20
NY, NZ, NE = 4, 16, 8
GROUP = 6
NSEL = 8
FEAT = 96
WIDE = NY * FEAT
TOKB = 128
ROWS = 2 * CAP
FIRST = -1e4
EPS = 1e-05
R_W = FEAT
R_K = R_W + GROUP * FEAT
R_V = R_K + 4 * BLK
R_ALL = R_V + 4 * BLK
L_ROUTER, L_SQ, L_GAIN = 64, 72, 72
BF, F32 = jnp.bfloat16, jnp.float32
NT = (((1,), (1,)), ((), ()))


def call(body, out_shape, n_in, smem=(), scratch=(), blocks=None):
    vmem = pl.BlockSpec(memory_space=pltpu.VMEM)
    specs = [pl.BlockSpec(memory_space=pltpu.SMEM) if i in smem else vmem for i in range(n_in)]
    return pl.pallas_call(
        body,
        out_shape=out_shape,
        in_specs=specs,
        out_specs=jax.tree.map(lambda _: vmem, out_shape),
        scratch_shapes=list(scratch),
        compiler_params=pltpu.CompilerParams(vmem_limit_bytes=48 * 1024 * 1024),
    )


def lanes(rows, width=128):
    return lax.broadcasted_iota(jnp.int32, (rows, width), 1)


def pack_body(k_ref, v_ref, w_ref, xt_ref, r_ref, g_ref, o_ref):
    gain = g_ref[...]
    hi = gain.astype(BF).astype(F32)
    mid = (gain - hi).astype(BF).astype(F32)
    lo = gain - hi - mid
    lane = lanes(FEAT)
    misc = xt_ref[...].astype(F32) + r_ref[...].astype(F32)
    misc = jnp.where(lane == L_GAIN, hi, misc)
    misc = jnp.where(lane == L_GAIN + 1, mid, misc)
    misc = jnp.where(lane == L_GAIN + 2, lo, misc).astype(BF)
    for y in range(NY):
        o_ref[y, 0:FEAT, :] = misc
        for g in range(GROUP):
            o_ref[y, R_W + g * FEAT : R_W + (g + 1) * FEAT, :] = w_ref[:, g * 128 : (g + 1) * 128]
        o_ref[y, R_K : R_K + 512, :] = k_ref[...]
        o_ref[y, R_V : R_V + 512, :] = v_ref[...]


def attend_body(s_ref, kv_ref, q_ref, o_ref, acc_ref, m_ref, l_ref):
    acc_ref[...] = jnp.zeros_like(acc_ref)
    l_ref[...] = jnp.zeros_like(l_ref)
    m_ref[...] = jnp.full(m_ref.shape, FIRST, F32)
    here = s_ref[NSEL]
    for i in range(NSEL):
        block = s_ref[i]
        owner = block >> 2

        @pl.when((owner & (NZ - 1)) == here)
        def _():
            row = owner >> 4
            start = pl.multiple_of((block & 3) * BLK, BLK)
            keys = kv_ref[row, pl.ds(R_K + start, BLK), :]
            values = kv_ref[row, pl.ds(R_V + start, BLK), :]
            query = jnp.concatenate(
                [q_ref[:, g * HD : (g + 1) * HD] for g in range(GROUP)], axis=0
            )
            s = lax.dot_general(query, keys, NT, preferred_element_type=F32) * HD ** (-0.5)
            old = m_ref[...]
            new = jnp.maximum(old, jnp.max(s, axis=1, keepdims=True))
            p = jnp.exp(s - new).astype(BF)
            keep = jnp.exp(old - new)
            l_ref[...] = l_ref[...] * keep + jnp.sum(p.astype(F32), axis=1, keepdims=True)
            acc_ref[...] = acc_ref[...] * keep + jnp.dot(p, values, preferred_element_type=F32)
            m_ref[...] = new

    lane = lanes(TOKB)
    stats = jnp.zeros((TOKB, 128), F32)
    for g in range(GROUP):
        rows = slice(g * TOKB, (g + 1) * TOKB)
        m, l = m_ref[rows, :], l_ref[rows, :]
        o_ref[:, g * HD : (g + 1) * HD] = (acc_ref[rows, :] / jnp.where(l > 0, l, 1.0)).astype(BF)
        near = m.astype(BF).astype(F32)
        total = l * jnp.exp(m - near)
        high = total.astype(BF).astype(F32)
        stats = jnp.where(lane == g, near, stats)
        stats = jnp.where(lane == 8 + g, high, stats)
        stats = jnp.where(lane == 16 + g, total - high, stats)
    o_ref[:, GROUP * HD :] = stats.astype(BF)


def merge_body(r_ref, o_ref):
    got = r_ref[...].astype(F32)
    stats = got[:, :, GROUP * HD :]
    for g in range(GROUP):
        m = stats[:, :, g : g + 1]
        l = stats[:, :, 8 + g : 9 + g] + stats[:, :, 16 + g : 17 + g]
        weight = l * jnp.exp(m - jnp.max(m, axis=0, keepdims=True))
        top = jnp.sum(weight * got[:, :, g * HD : (g + 1) * HD], axis=0)
        out = (top / jnp.sum(weight, axis=0)).astype(BF)
        o_ref[:, :, g * HD : (g + 1) * HD] = jnp.broadcast_to(out[None], (NZ,) + out.shape)


def project_body(s_ref, a_ref, w_ref, id_ref, o_ref):
    y, e = s_ref[0], s_ref[1]
    total = jnp.zeros((TOKB, WIDE), F32)
    for g in range(GROUP):
        w = jnp.concatenate(
            [w_ref[n, R_W + g * FEAT : R_W + (g + 1) * FEAT, :] for n in range(NY)], axis=0
        )
        total += lax.dot_general(
            a_ref[:, g * 128 : (g + 1) * 128], w, NT, preferred_element_type=F32
        )
    misc = jnp.concatenate([w_ref[n, 0:FEAT, :] for n in range(NY)], axis=0)
    row = lax.broadcasted_iota(jnp.int32, (TOKB, 128), 0)
    mine = (row == lanes(TOKB) + (e & 1) * 64) & (lanes(TOKB) < 64) & ((e >> 1) == y)
    total += lax.dot_general(
        jnp.where(mine, 1.0, 0.0).astype(BF), misc, NT, preferred_element_type=F32
    )
    out = total.astype(BF)
    for n in range(NE):
        o_ref[n, 0:TOKB, :] = out
        o_ref[n, TOKB:, :] = id_ref[...]


def pick_body(s_ref, r_ref, w_ref, x_ref, loc_ref):
    y, e = s_ref[0], s_ref[1]
    res = r_ref[0, 0:TOKB, :].astype(F32)
    for n in range(1, NE):
        res += r_ref[n, 0:TOKB, :].astype(F32)
    misc = jnp.concatenate([w_ref[n, 0:FEAT, :] for n in range(NY)], axis=0)
    sub = lax.broadcasted_iota(jnp.int32, (8, 128), 0)
    take = (lanes(8) == L_GAIN + sub) & (sub < 3)
    gain = lax.dot_general(
        jnp.where(take, 1.0, 0.0).astype(BF), misc, NT, preferred_element_type=F32
    )
    gain = jnp.sum(gain, axis=0, keepdims=True)
    scaled = res * gain
    sq = jnp.sum(res * res, axis=1, keepdims=True)
    high = scaled.astype(BF)
    low = (scaled - high.astype(F32)).astype(BF)
    logits = jnp.dot(high, misc, preferred_element_type=F32) + jnp.dot(
        low, misc, preferred_element_type=F32
    )
    lane = lanes(TOKB)
    stats = jnp.where((lane >= L_ROUTER) & (lane < L_ROUTER + 8), logits, 0.0)
    stats = jnp.where(lane == L_SQ, sq, stats)
    stats_high = stats.astype(BF).astype(F32)
    both = (stats_high + pltpu.roll(stats - stats_high, 64, 1)).astype(BF)
    ids = r_ref[2 * y, TOKB:, :].astype(F32) + r_ref[2 * y + 1, TOKB:, :].astype(F32)
    id0, id1 = ids[0:1, 0:128], ids[0:1, 128:256]
    slot0, slot1 = ids[1:2, 0:128], ids[1:2, 128:256]
    want = lax.broadcasted_iota(jnp.int32, (ROWS, 128), 0).astype(F32)
    base = jnp.where(lanes(1) >= 64, float(CAP), 0.0)
    me = e.astype(F32)
    m0 = jnp.where((id0 == me) & (slot0 + base == want), 1.0, 0.0)
    m1 = jnp.where((id1 == me) & (slot1 + base == want), 1.0, 0.0)
    choose = (m0 + m1).astype(BF)
    other = jnp.sum(m0 * id1 + m1 * id0, axis=1, keepdims=True)
    first = jnp.sum(m0, axis=1, keepdims=True)
    x_ref[:, 0:WIDE] = jnp.dot(choose, high, preferred_element_type=F32).astype(BF)
    x_ref[:, WIDE:] = jnp.dot(choose, both, preferred_element_type=F32).astype(BF)
    res_high = res.astype(BF)
    res_low = (res - res_high.astype(F32)).astype(BF)
    loc_ref[:, 0:WIDE] = jnp.dot(choose, res_high, preferred_element_type=F32)
    loc_ref[:, WIDE : 2 * WIDE] = jnp.dot(choose, res_low, preferred_element_type=F32)
    side = lanes(ROWS)
    loc_ref[:, 2 * WIDE :] = jnp.where(side == 0, other, jnp.where(side == 1, first, 0.0))


def norm_body(s_ref, g_ref, loc_ref, o_ref):
    e = s_ref[1]
    stats = g_ref[0, :, WIDE:].astype(F32)
    for z in range(1, NZ):
        stats += g_ref[z, :, WIDE:].astype(F32)
    stats = stats + pltpu.roll(stats, 64, 1)
    inverse = lax.rsqrt(stats[:, L_SQ : L_SQ + 1] / D + EPS)
    other = loc_ref[:, 2 * WIDE : 2 * WIDE + 1]
    first = loc_ref[:, 2 * WIDE + 1 : 2 * WIDE + 2]
    lane = lanes(ROWS)
    mine = jnp.sum(jnp.where(lane == L_ROUTER + e, stats, 0.0), axis=1, keepdims=True)
    rival = jnp.where(lane.astype(F32) == other + float(L_ROUTER), stats, 0.0)
    rival = jnp.sum(rival, axis=1, keepdims=True)
    gate = 1.0 / (1.0 + jnp.exp((rival - mine) * inverse))
    gate_high = gate.astype(BF).astype(F32)
    for z in range(NZ):
        normed = (g_ref[z, :, 0:WIDE].astype(F32) * inverse).astype(BF)
        for n in range(NY):
            o_ref[n, :, z * WIDE : (z + 1) * WIDE] = normed
    zeros = jnp.zeros((ROWS, 128 - FEAT), F32)
    tail = lanes(ROWS, 128 - FEAT)
    for n in range(NY):
        o_ref[n, :, D : D + FEAT] = loc_ref[:, n * FEAT : (n + 1) * FEAT].astype(BF)
        o_ref[n, :, D + 128 : D + 128 + FEAT] = loc_ref[
            :, WIDE + n * FEAT : WIDE + (n + 1) * FEAT
        ].astype(BF)
        o_ref[n, :, D + FEAT : D + 128] = jnp.where(
            tail == 0, gate_high, jnp.where(tail == 1, first, zeros)
        ).astype(BF)
        o_ref[n, :, D + 128 + FEAT :] = jnp.where(tail == 0, gate - gate_high, zeros).astype(BF)


def lift_body(x_ref, wg_ref, wu_ref, o_ref):
    gate = jnp.zeros((NY * ROWS, 128), F32)
    lift = jnp.zeros((NY * ROWS, 128), F32)
    for z in range(NZ):
        x = x_ref[:, z * WIDE : (z + 1) * WIDE]
        wg = jnp.concatenate([wg_ref[n, z] for n in range(NY)], axis=0)
        wu = jnp.concatenate([wu_ref[n, z] for n in range(NY)], axis=0)
        gate += jnp.dot(x, wg, preferred_element_type=F32)
        lift += jnp.dot(x, wu, preferred_element_type=F32)
    o_ref[...] = (gate / (1.0 + jnp.exp(-gate)) * lift).astype(BF)


def down_body(h_ref, w_ref, x_ref, o_ref):
    total = jnp.zeros((NY * ROWS, FEAT), F32)
    for n in range(NY):
        for z in range(0, NZ, 4):
            h = jnp.concatenate([h_ref[n, z + i] for i in range(4)], axis=1)
            at = (n * NZ + z) * 128
            total += lax.dot_general(
                h, w_ref[:, at : at + 512], NT, preferred_element_type=F32
            )
    rounded = total.astype(BF).astype(F32)
    high = x_ref[:, 0:128].astype(F32)
    low = x_ref[:, 128:256].astype(F32)
    gate = high[:, FEAT : FEAT + 1] + low[:, FEAT : FEAT + 1]
    first = high[:, FEAT + 1 : FEAT + 2]
    residual = high[:, 0:FEAT] + low[:, 0:FEAT]
    o_ref[...] = gate * rounded + jnp.where(first > 0.5, residual, 0.0)


def swap(x, axis):
    return lax.all_to_all(x, axis, split_axis=0, concat_axis=0, tiled=True)


def shape(*dims, dtype=BF):
    return jax.ShapeDtypeStruct(dims, dtype)


def per_device(
    x_resid,
    queries,
    keys,
    values,
    pattern,
    global_blocks,
    out_weight,
    norm_gain,
    router,
    expert_ids,
    expert_slots,
    w_gate,
    w_up,
    w_down,
):
    y, z, e = lax.axis_index("y"), lax.axis_index("z"), lax.axis_index("exp")
    place = jnp.stack([y, e]).astype(jnp.int32)
    listed = jnp.concatenate([pattern[y], global_blocks, z[None].astype(jnp.int32)])

    pairs = jnp.concatenate([expert_ids.T, expert_slots.T], axis=0).astype(BF)
    blank = jnp.zeros_like(pairs)
    pairs = jnp.where(
        (e & 1) == 0,
        jnp.concatenate([pairs, blank], axis=1),
        jnp.concatenate([blank, pairs], axis=1),
    )
    id_rows = jnp.pad(pairs.reshape(2, 256), ((0, 14), (0, 128)))

    packed = call(pack_body, shape(NY, R_ALL, 128), 6)(
        keys,
        values,
        out_weight.T,
        jnp.pad(x_resid.T, ((0, 0), (0, 64))),
        jnp.pad(router, ((0, 0), (L_ROUTER, 128 - L_ROUTER - 8))),
        norm_gain[:, None],
    )
    column = swap(packed, "y")
    block_queries = swap(jnp.broadcast_to(queries[None], (NZ,) + queries.shape), "z")

    partial = call(
        attend_body,
        shape(TOKB, (GROUP + 1) * HD),
        3,
        smem=(0,),
        scratch=[pltpu.VMEM((GROUP * TOKB, 128), F32)] * 3,
    )(listed, column, block_queries.reshape(TOKB, GROUP * HD))
    partial = swap(partial.reshape(NZ, TOKB // NZ, (GROUP + 1) * HD), "z")
    attention = call(merge_body, shape(NZ, TOKB // NZ, GROUP * HD), 1)(partial)
    attention = swap(attention, "z").reshape(TOKB, GROUP * HD)

    products = call(project_body, shape(NE, TOKB + 16, WIDE), 4, smem=(0,))(
        place, attention, column[:, :R_K], id_rows
    )
    products = swap(products, "exp")
    rows, local = call(
        pick_body,
        (shape(ROWS, WIDE + 128), shape(ROWS, 2 * WIDE + 128, dtype=F32)),
        3,
        smem=(0,),
    )(place, products, column[:, :R_W])
    gathered = lax.all_gather(rows, "z", axis=0)
    normed = call(norm_body, shape(NY, ROWS, D + 256), 3, smem=(0,))(place, gathered, local)
    normed = swap(normed, "y").reshape(NY * ROWS, D + 256)

    hidden = call(lift_body, shape(NY * ROWS, 128), 3)(
        normed, w_gate.reshape(NY, NZ, FEAT, 128), w_up.reshape(NY, NZ, FEAT, 128)
    )
    hidden = lax.all_gather(hidden, "z", axis=0)
    hidden = swap(jnp.broadcast_to(hidden[None], (NY,) + hidden.shape), "y")
    hidden = hidden.reshape(NY, NZ, NY * ROWS, 128)
    out = call(down_body, shape(NY * ROWS, FEAT, dtype=F32), 3)(
        hidden, w_down[0].T, normed[:, D:]
    )
    back = swap(out.reshape(NE, CAP, FEAT), "exp").reshape(NE * CAP, FEAT)
    flat = expert_ids * CAP + expert_slots
    at = jnp.arange(NE * CAP, dtype=jnp.int32)[None, :]
    both = (flat[:, :1] == at).astype(F32) + (flat[:, 1:] == at).astype(F32)
    return jnp.dot(both, back, precision=lax.Precision.HIGHEST).astype(BF)


def solution(mesh):
    inner = Mesh(mesh.devices.reshape(NY, NZ, NE), ("y", "z", "exp"))
    ctx = ("y", "z")
    in_specs = (
        P("exp", ctx),
        P(ctx, "exp"),
        P(ctx, "exp"),
        P(ctx, "exp"),
        P(),
        P(),
        P("exp", ctx),
        P(ctx),
        P(ctx, None),
        P("exp", None),
        P("exp", None),
        P("exp", None, ctx),
        P("exp", None, ctx),
        P("exp", None, ctx),
    )
    return jax.shard_map(
        per_device, mesh=inner, in_specs=in_specs, out_specs=P("exp", ctx), check_vma=False
    )
```

```python
import jax
import jax.numpy as jnp
from jax import lax
from jax.experimental import pallas as pl
from jax.experimental.pallas import tpu as pltpu
from jax.sharding import Mesh, PartitionSpec as P

D = 6144
HD = 128
BLK = 128
CAP = 20
NY, NZ, NE = 4, 16, 8
GROUP = 6
NSEL = 8
FEAT = 96
WIDE = NY * FEAT
TOKB = 128
ROWS = 2 * CAP
FIRST = -1e4
EPS = 1e-05
STATS = 128
R_W = FEAT
R_K = R_W + GROUP * FEAT
R_V = R_K + 4 * BLK
R_ALL = R_V + 4 * BLK
L_ROUTER, L_SQ, L_GAIN = 64, 72, 72
BF, F32 = jnp.bfloat16, jnp.float32
NT = (((1,), (1,)), ((), ()))


def call(body, out_shape, specs, scratch=(), prefetch=0, mib=40):
    params = pltpu.CompilerParams(vmem_limit_bytes=mib * 1024 * 1024)
    outs = jax.tree.map(lambda _: pl.BlockSpec(memory_space=pltpu.VMEM), out_shape)
    grid = pltpu.PrefetchScalarGridSpec(
        num_scalar_prefetch=prefetch,
        grid=(1,),
        in_specs=specs,
        out_specs=outs,
        scratch_shapes=list(scratch),
    )
    return pl.pallas_call(body, out_shape=out_shape, grid_spec=grid, compiler_params=params)


VM = pl.BlockSpec(memory_space=pltpu.VMEM)


def part(*block, at=None):
    at = (0,) * len(block) if at is None else at
    return pl.BlockSpec(block, lambda i, *s: at)


def lanes(rows, width=128):
    return lax.broadcasted_iota(jnp.int32, (rows, width), 1)


def pack_body(k_ref, v_ref, w_ref, x_ref, r_ref, g_ref, o_ref):
    gain = g_ref[...]
    hi = gain.astype(BF).astype(F32)
    mid = (gain - hi).astype(BF).astype(F32)
    lo = gain - hi - mid
    sub = lax.broadcasted_iota(jnp.int32, (8, FEAT), 0)
    gains = jnp.where(sub == 0, hi, jnp.where(sub == 1, mid, jnp.where(sub == 2, lo, 0.0)))
    blank = jnp.zeros((48, FEAT), F32)
    rows = jnp.concatenate([x_ref[...].astype(F32), r_ref[...].astype(F32), gains, blank], axis=0)
    eye = lax.broadcasted_iota(jnp.int32, (FEAT, FEAT), 0) == lanes(FEAT, FEAT)
    misc = lax.dot_general(
        jnp.where(eye, 1.0, 0.0).astype(BF), rows.astype(BF), NT, preferred_element_type=F32
    ).astype(BF)
    for y in range(NY):
        o_ref[y, 0:FEAT, :] = misc
        for g in range(GROUP):
            o_ref[y, R_W + g * FEAT : R_W + (g + 1) * FEAT, :] = w_ref[:, g * 128 : (g + 1) * 128]
        o_ref[y, R_K : R_K + 512, :] = k_ref[...]
        o_ref[y, R_V : R_V + 512, :] = v_ref[...]


def stacked(ref, start):
    return jnp.concatenate([ref[n, start : start + FEAT, :] for n in range(NY)], axis=0)


def attend_body(s_ref, kv_ref, q_ref, o_ref, acc_ref, m_ref, l_ref):
    acc_ref[...] = jnp.zeros_like(acc_ref)
    l_ref[...] = jnp.zeros_like(l_ref)
    m_ref[...] = jnp.full(m_ref.shape, FIRST, F32)
    here = s_ref[NSEL]
    for i in range(NSEL):
        block = s_ref[i]
        owner = block >> 2

        @pl.when((owner & (NZ - 1)) == here)
        def _():
            row = owner >> 4
            start = pl.multiple_of((block & 3) * BLK, BLK)
            keys = kv_ref[row, pl.ds(R_K + start, BLK), :]
            values = kv_ref[row, pl.ds(R_V + start, BLK), :]
            query = jnp.concatenate(
                [q_ref[:, g * HD : (g + 1) * HD] for g in range(GROUP)], axis=0
            )
            s = lax.dot_general(query, keys, NT, preferred_element_type=F32) * HD ** (-0.5)
            old = m_ref[...]
            new = jnp.maximum(old, jnp.max(s, axis=1, keepdims=True))
            p = jnp.exp(s - new).astype(BF)
            keep = jnp.exp(old - new)
            l_ref[...] = l_ref[...] * keep + jnp.sum(p.astype(F32), axis=1, keepdims=True)
            acc_ref[...] = acc_ref[...] * keep + jnp.dot(p, values, preferred_element_type=F32)
            m_ref[...] = new

    lane = lanes(TOKB)
    stats = jnp.zeros((TOKB, 128), F32)
    for g in range(GROUP):
        rows = slice(g * TOKB, (g + 1) * TOKB)
        m, l = m_ref[rows, :], l_ref[rows, :]
        o_ref[:, g * HD : (g + 1) * HD] = (acc_ref[rows, :] / jnp.where(l > 0, l, 1.0)).astype(BF)
        near = m.astype(BF).astype(F32)
        total = l * jnp.exp(m - near)
        high = total.astype(BF).astype(F32)
        stats = jnp.where(lane == g, near, stats)
        stats = jnp.where(lane == 8 + g, high, stats)
        stats = jnp.where(lane == 16 + g, total - high, stats)
    o_ref[:, GROUP * HD :] = stats.astype(BF)


def merge_body(r_ref, o_ref):
    got = r_ref[...].astype(F32)
    stats = got[:, :, GROUP * HD :]
    for g in range(GROUP):
        m = stats[:, :, g : g + 1]
        l = stats[:, :, 8 + g : 9 + g] + stats[:, :, 16 + g : 17 + g]
        weight = l * jnp.exp(m - jnp.max(m, axis=0, keepdims=True))
        top = jnp.sum(weight * got[:, :, g * HD : (g + 1) * HD], axis=0)
        out = (top / jnp.sum(weight, axis=0)).astype(BF)
        o_ref[:, :, g * HD : (g + 1) * HD] = jnp.broadcast_to(out[None], (NZ,) + out.shape)


def project_body(s_ref, a_ref, w_ref, ids_ref, o_ref):
    y, e = s_ref[0], s_ref[1]
    total = jnp.zeros((TOKB, WIDE), F32)
    for g in range(GROUP):
        total += lax.dot_general(
            a_ref[:, g * 128 : (g + 1) * 128],
            stacked(w_ref, R_W + g * FEAT),
            NT,
            preferred_element_type=F32,
        )
    row = lax.broadcasted_iota(jnp.int32, (TOKB, 128), 0)
    mine = (row == lanes(TOKB) + (e & 1) * 64) & (lanes(TOKB) < 64) & ((e >> 1) == y)
    total += lax.dot_general(
        jnp.where(mine, 1.0, 0.0).astype(BF),
        stacked(w_ref, 0),
        NT,
        preferred_element_type=F32,
    )
    out = total.astype(BF)
    for n in range(NE):
        o_ref[n, 0:TOKB, :] = out
        o_ref[n, TOKB:, :] = ids_ref[...]


def pick_body(s_ref, r_ref, w_ref, x_ref, res_ref, side_ref):
    y, e = s_ref[0], s_ref[1]
    total = r_ref[0, 0:TOKB, :].astype(F32)
    for n in range(1, NE):
        total += r_ref[n, 0:TOKB, :].astype(F32)
    ids = r_ref[2 * y, TOKB:, :].astype(F32) + r_ref[2 * y + 1, TOKB:, :].astype(F32)
    id0, id1 = ids[0:1, 0:128], ids[0:1, 128:256]
    base = jnp.where(lanes(1) >= 64, float(CAP), 0.0)
    want = lax.broadcasted_iota(jnp.int32, (ROWS, 128), 0).astype(F32)
    me = e.astype(F32)
    m0 = jnp.where((id0 == me) & (ids[1:2, 0:128] + base == want), 1.0, 0.0)
    m1 = jnp.where((id1 == me) & (ids[1:2, 128:256] + base == want), 1.0, 0.0)
    choose = (m0 + m1).astype(BF)
    other = jnp.sum(m0 * id1 + m1 * id0, axis=1, keepdims=True)
    first = jnp.sum(m0, axis=1, keepdims=True)
    total_high = total.astype(BF)
    total_low = (total - total_high.astype(F32)).astype(BF)
    res = jnp.dot(choose, total_high, preferred_element_type=F32) + jnp.dot(
        choose, total_low, preferred_element_type=F32
    )
    misc = stacked(w_ref, 0)
    sub = lax.broadcasted_iota(jnp.int32, (8, 128), 0)
    take = (lanes(8) == L_GAIN + sub) & (sub < 3)
    gain = lax.dot_general(
        jnp.where(take, 1.0, 0.0).astype(BF), misc, NT, preferred_element_type=F32
    )
    scaled = res * jnp.sum(gain, axis=0, keepdims=True)
    sq = jnp.sum(res * res, axis=1, keepdims=True)
    high = scaled.astype(BF)
    low = (scaled - high.astype(F32)).astype(BF)
    logits = jnp.dot(high, misc, preferred_element_type=F32) + jnp.dot(
        low, misc, preferred_element_type=F32
    )
    lane = lanes(ROWS)
    stats = jnp.where((lane >= L_ROUTER) & (lane < L_ROUTER + 8), logits, 0.0)
    stats = jnp.where(lane == L_SQ, sq, stats)
    stats_high = stats.astype(BF).astype(F32)
    x_ref[:, 0:WIDE] = high
    x_ref[:, WIDE:] = (stats_high + pltpu.roll(stats - stats_high, 64, 1)).astype(BF)
    side_ref[...] = jnp.broadcast_to(other, (ROWS, 128))
    kept = jnp.where(first > 0.5, res, 0.0)
    for n in range(NY):
        for i in range(2):
            rows = slice(i * CAP, (i + 1) * CAP)
            res_ref[n, i] = kept[rows, n * FEAT : (n + 1) * FEAT]


def norm_body(s_ref, g_ref, side_ref, o_ref):
    e = s_ref[1]
    stats = g_ref[0, :, WIDE:].astype(F32)
    for z in range(1, NZ):
        stats += g_ref[z, :, WIDE:].astype(F32)
    stats = stats + pltpu.roll(stats, 64, 1)
    inverse = lax.rsqrt(stats[:, L_SQ : L_SQ + 1] / D + EPS)
    lane = lanes(ROWS)
    mine = jnp.sum(jnp.where(lane == L_ROUTER + e, stats, 0.0), axis=1, keepdims=True)
    rival = jnp.where(lane.astype(F32) == side_ref[...] + float(L_ROUTER), stats, 0.0)
    rival = jnp.sum(rival, axis=1, keepdims=True)
    gate = 1.0 / (1.0 + jnp.exp((rival - mine) * inverse))
    gate_high = gate.astype(BF).astype(F32)
    gates = jnp.where(lane == 0, gate_high, jnp.where(lane == 1, gate - gate_high, 0.0))
    gates = gates.astype(BF)
    for z in range(NZ):
        normed = (g_ref[z, :, 0:WIDE].astype(F32) * inverse).astype(BF)
        for n in range(NY):
            o_ref[n, :, z * WIDE : (z + 1) * WIDE] = normed
    for n in range(NY):
        o_ref[n, :, D:] = gates


def lift_body(x_ref, wg_ref, wu_ref, o_ref):
    gate = jnp.zeros((NY * ROWS, 128), F32)
    lift = jnp.zeros((NY * ROWS, 128), F32)
    for z in range(NZ):
        x = x_ref[:, z * WIDE : (z + 1) * WIDE]
        wg = jnp.concatenate([wg_ref[n, z] for n in range(NY)], axis=0)
        wu = jnp.concatenate([wu_ref[n, z] for n in range(NY)], axis=0)
        gate += jnp.dot(x, wg, preferred_element_type=F32)
        lift += jnp.dot(x, wu, preferred_element_type=F32)
    o_ref[...] = (gate / (1.0 + jnp.exp(-gate)) * lift).astype(BF)


def down_body(s_ref, h_ref, w_ref, gates_ref, res_ref, o_ref):
    y = s_ref[0]
    gates = gates_ref[...].astype(F32)
    gate = gates[:, 0:1] + gates[:, 1:2]
    for n in range(NY):
        total = jnp.zeros((NY * ROWS, FEAT), F32)
        for z in range(0, NZ, 4):
            h = jnp.concatenate([h_ref[z + i] for i in range(4)], axis=1)
            w = w_ref[n, :, z * 128 : (z + 4) * 128]
            total += lax.dot_general(h, w, NT, preferred_element_type=F32)
        total = gate * total
        for i in range(NE):
            o_ref[n, i] = total[i * CAP : (i + 1) * CAP, :]
        for i in range(2):
            o_ref[n, 2 * y + i] += res_ref[n, i]


def swap(x, axis):
    return lax.all_to_all(x, axis, split_axis=0, concat_axis=0, tiled=True)


def shape(*dims, dtype=BF):
    return jax.ShapeDtypeStruct(dims, dtype)


def per_device(
    x_resid,
    queries,
    keys,
    values,
    pattern,
    global_blocks,
    out_weight,
    norm_gain,
    router,
    expert_ids,
    expert_slots,
    w_gate,
    w_up,
    w_down,
):
    y, z, e = lax.axis_index("y"), lax.axis_index("z"), lax.axis_index("exp")
    place = jnp.stack([y, e]).astype(jnp.int32)
    listed = jnp.concatenate([pattern[y], global_blocks, z[None].astype(jnp.int32)])

    pairs = jnp.concatenate([expert_ids.T, expert_slots.T], axis=0).astype(BF)
    blank = jnp.zeros_like(pairs)
    pairs = jnp.where(
        (e & 1) == 0,
        jnp.concatenate([pairs, blank], axis=1),
        jnp.concatenate([blank, pairs], axis=1),
    )
    id_rows = jnp.pad(pairs.reshape(2, 256), ((0, 14), (0, 128)))

    inputs = (keys, values, out_weight.T, x_resid, router.T, norm_gain[None])
    packed = call(
        pack_body, shape(NY, R_ALL, 128), [part(*a.shape) for a in inputs], mib=56
    )(*inputs)
    column = swap(packed, "y")
    block_queries = lax.all_gather(queries, "z", axis=0, tiled=True)

    partial = call(
        attend_body,
        shape(TOKB, (GROUP + 1) * HD),
        [VM] * 2,
        scratch=[pltpu.VMEM((GROUP * TOKB, 128), F32)] * 3,
        prefetch=1,
    )(listed, column, block_queries)
    partial, down = lax.optimization_barrier((partial, w_down[0].T))
    down = down.reshape(FEAT, NY, NZ * 128).swapaxes(0, 1)
    partial = swap(partial.reshape(NZ, TOKB // NZ, (GROUP + 1) * HD), "z")
    attention = call(merge_body, shape(NZ, TOKB // NZ, GROUP * HD), [VM])(partial)
    attention = swap(attention, "z").reshape(TOKB, GROUP * HD)
    products = call(
        project_body,
        shape(NE, TOKB + 16, WIDE),
        [VM, part(NY, R_K, 128), VM],
        prefetch=1,
    )(place, attention, column, id_rows)
    products = swap(products, "exp")
    rows, residual, side = call(
        pick_body,
        (
            shape(ROWS, WIDE + STATS),
            shape(NY, 2, CAP, FEAT, dtype=F32),
            shape(ROWS, 128, dtype=F32),
        ),
        [VM, part(NY, FEAT, 128)],
        prefetch=1,
    )(place, products, column)
    rows, down = lax.optimization_barrier((rows, down))
    down_column = swap(down, "y")
    gathered = lax.all_gather(rows, "z", axis=0)
    gathered, down_column = lax.optimization_barrier((gathered, down_column))
    normed = call(norm_body, shape(NY, ROWS, D + 128), [VM, VM], prefetch=1)(
        place, gathered, side
    )
    normed = swap(normed, "y").reshape(NY * ROWS, D + 128)

    hidden = call(lift_body, shape(NY * ROWS, 128), [VM] * 3)(
        normed, w_gate.reshape(NY, NZ, FEAT, 128), w_up.reshape(NY, NZ, FEAT, 128)
    )
    hidden = lax.all_gather(hidden, "z", axis=0)
    out = call(
        down_body,
        shape(NY, NE, CAP, FEAT, dtype=F32),
        [
            VM,
            VM,
            part(NY * ROWS, 128, at=(0, D // 128)),
            VM,
        ],
        prefetch=1,
    )(place, hidden, down_column, normed, residual)
    back = swap(out.reshape(NY * NE, CAP, FEAT), ("y", "exp")).reshape(NY * NE * CAP, FEAT)
    flat = expert_ids * CAP + expert_slots
    at = jnp.arange(NY * NE * CAP, dtype=jnp.int32)[None, :] % (NE * CAP)
    both = (flat[:, :1] == at).astype(F32) + (flat[:, 1:] == at).astype(F32)
    return jnp.dot(both, back, precision=lax.Precision.HIGHEST).astype(BF)


def solution(mesh):
    inner = Mesh(mesh.devices.reshape(NY, NZ, NE), ("y", "z", "exp"))
    ctx = ("y", "z")
    in_specs = (
        P("exp", ctx),
        P(ctx, "exp"),
        P(ctx, "exp"),
        P(ctx, "exp"),
        P(),
        P(),
        P("exp", ctx),
        P(ctx),
        P(ctx, None),
        P("exp", None),
        P("exp", None),
        P("exp", None, ctx),
        P("exp", None, ctx),
        P("exp", None, ctx),
    )
    return jax.shard_map(
        per_device, mesh=inner, in_specs=in_specs, out_specs=P("exp", ctx), check_vma=False
    )
```

```python
import jax
import jax.numpy as jnp
from jax import lax
from jax.experimental import pallas as pl
from jax.experimental.pallas import tpu as pltpu
from jax.sharding import Mesh, PartitionSpec as P

D = 6144
HD = 128
BLK = 128
CAP = 20
NY, NZ, NE = 4, 16, 8
GROUP = 6
NSEL = 8
FEAT = 96
WIDE = NY * FEAT
TOKB = 128
ROWS = 2 * CAP
FIRST = -1e4
EPS = 1e-05
STATS = 128
R_W = FEAT
R_K = R_W + GROUP * FEAT
R_V = R_K + 4 * BLK
R_ALL = R_V + 4 * BLK
L_ROUTER, L_SQ, L_GAIN = 64, 72, 72
BF, F32 = jnp.bfloat16, jnp.float32
NT = (((1,), (1,)), ((), ()))


def call(body, out_shape, specs, scratch=(), prefetch=0, mib=40):
    params = pltpu.CompilerParams(vmem_limit_bytes=mib * 1024 * 1024)
    outs = jax.tree.map(lambda _: pl.BlockSpec(memory_space=pltpu.VMEM), out_shape)
    grid = pltpu.PrefetchScalarGridSpec(
        num_scalar_prefetch=prefetch,
        grid=(1,),
        in_specs=specs,
        out_specs=outs,
        scratch_shapes=list(scratch),
    )
    return pl.pallas_call(body, out_shape=out_shape, grid_spec=grid, compiler_params=params)


VM = pl.BlockSpec(memory_space=pltpu.VMEM)


def part(*block, at=None):
    at = (0,) * len(block) if at is None else at
    return pl.BlockSpec(block, lambda i, *s: at)


def lanes(rows, width=128):
    return lax.broadcasted_iota(jnp.int32, (rows, width), 1)


def pack_body(k_ref, v_ref, w_ref, x_ref, r_ref, g_ref, o_ref):
    gain = g_ref[...]
    hi = gain.astype(BF).astype(F32)
    mid = (gain - hi).astype(BF).astype(F32)
    lo = gain - hi - mid
    sub = lax.broadcasted_iota(jnp.int32, (8, FEAT), 0)
    gains = jnp.where(sub == 0, hi, jnp.where(sub == 1, mid, jnp.where(sub == 2, lo, 0.0)))
    blank = jnp.zeros((48, FEAT), F32)
    rows = jnp.concatenate([x_ref[...].astype(F32), r_ref[...].astype(F32), gains, blank], axis=0)
    eye = lax.broadcasted_iota(jnp.int32, (FEAT, FEAT), 0) == lanes(FEAT, FEAT)
    misc = lax.dot_general(
        jnp.where(eye, 1.0, 0.0).astype(BF), rows.astype(BF), NT, preferred_element_type=F32
    ).astype(BF)
    for y in range(NY):
        o_ref[y, 0:FEAT, :] = misc
        for g in range(GROUP):
            o_ref[y, R_W + g * FEAT : R_W + (g + 1) * FEAT, :] = w_ref[:, g * 128 : (g + 1) * 128]
        o_ref[y, R_K : R_K + 512, :] = k_ref[...]
        o_ref[y, R_V : R_V + 512, :] = v_ref[...]


def stacked(ref, start):
    return jnp.concatenate([ref[n, start : start + FEAT, :] for n in range(NY)], axis=0)


def attend_body(s_ref, kv_ref, q_ref, o_ref, acc_ref, m_ref, l_ref):
    acc_ref[...] = jnp.zeros_like(acc_ref)
    l_ref[...] = jnp.zeros_like(l_ref)
    m_ref[...] = jnp.full(m_ref.shape, FIRST, F32)
    here = s_ref[NSEL]
    for i in range(NSEL):
        block = s_ref[i]
        owner = block >> 2

        @pl.when((owner & (NZ - 1)) == here)
        def _():
            row = owner >> 4
            start = pl.multiple_of((block & 3) * BLK, BLK)
            keys = kv_ref[row, pl.ds(R_K + start, BLK), :]
            values = kv_ref[row, pl.ds(R_V + start, BLK), :]
            query = jnp.concatenate(
                [q_ref[:, g * HD : (g + 1) * HD] for g in range(GROUP)], axis=0
            )
            s = lax.dot_general(query, keys, NT, preferred_element_type=F32) * HD ** (-0.5)
            old = m_ref[...]
            new = jnp.maximum(old, jnp.max(s, axis=1, keepdims=True))
            p = jnp.exp(s - new).astype(BF)
            keep = jnp.exp(old - new)
            l_ref[...] = l_ref[...] * keep + jnp.sum(p.astype(F32), axis=1, keepdims=True)
            acc_ref[...] = acc_ref[...] * keep + jnp.dot(p, values, preferred_element_type=F32)
            m_ref[...] = new

    lane = lanes(TOKB)
    stats = jnp.zeros((TOKB, 128), F32)
    for g in range(GROUP):
        rows = slice(g * TOKB, (g + 1) * TOKB)
        m, l = m_ref[rows, :], l_ref[rows, :]
        o_ref[:, g * HD : (g + 1) * HD] = (acc_ref[rows, :] / jnp.where(l > 0, l, 1.0)).astype(BF)
        near = m.astype(BF).astype(F32)
        total = l * jnp.exp(m - near)
        high = total.astype(BF).astype(F32)
        stats = jnp.where(lane == g, near, stats)
        stats = jnp.where(lane == 8 + g, high, stats)
        stats = jnp.where(lane == 16 + g, total - high, stats)
    o_ref[:, GROUP * HD :] = stats.astype(BF)


def merge_body(r_ref, o_ref):
    got = r_ref[...].astype(F32)
    stats = got[:, :, GROUP * HD :]
    for g in range(GROUP):
        m = stats[:, :, g : g + 1]
        l = stats[:, :, 8 + g : 9 + g] + stats[:, :, 16 + g : 17 + g]
        weight = l * jnp.exp(m - jnp.max(m, axis=0, keepdims=True))
        top = jnp.sum(weight * got[:, :, g * HD : (g + 1) * HD], axis=0)
        out = (top / jnp.sum(weight, axis=0)).astype(BF)
        o_ref[:, :, g * HD : (g + 1) * HD] = jnp.broadcast_to(out[None], (NZ,) + out.shape)


def slot_keys(ids_ref):
    ids = ids_ref[0].astype(F32) + ids_ref[1].astype(F32)
    id0, id1, slot0, slot1 = (ids[i : i + 1, :] for i in range(4))
    base = jnp.where(lanes(1) >= 64, float(CAP), 0.0)
    return id0 * ROWS + slot0 + base, id1 * ROWS + slot1 + base, id0, id1


def project_body(s_ref, a_ref, w_ref, ids_ref, o_ref):
    y, e = s_ref[0], s_ref[1]
    total = jnp.zeros((TOKB, WIDE), F32)
    for g in range(GROUP):
        total += lax.dot_general(
            a_ref[:, g * 128 : (g + 1) * 128],
            stacked(w_ref, R_W + g * FEAT),
            NT,
            preferred_element_type=F32,
        )
    row = lax.broadcasted_iota(jnp.int32, (TOKB, 128), 0)
    mine = (row == lanes(TOKB) + (e & 1) * 64) & (lanes(TOKB) < 64) & ((e >> 1) == y)
    total += lax.dot_general(
        jnp.where(mine, 1.0, 0.0).astype(BF),
        stacked(w_ref, 0),
        NT,
        preferred_element_type=F32,
    )
    key0, key1, _, _ = slot_keys(ids_ref)
    want = lax.broadcasted_iota(jnp.int32, (NE * ROWS, 128), 0).astype(F32)
    choose = jnp.where((key0 == want) | (key1 == want), 1.0, 0.0).astype(BF)
    o_ref[...] = jnp.dot(choose, total.astype(BF), preferred_element_type=F32).astype(BF)


def pick_body(s_ref, r_ref, w_ref, ids_ref, x_ref, res_ref, side_ref):
    e = s_ref[1]
    res = r_ref[0].astype(F32)
    for n in range(1, NE):
        res += r_ref[n].astype(F32)
    key0, key1, id0, id1 = slot_keys(ids_ref)
    want = (lax.broadcasted_iota(jnp.int32, (ROWS, 128), 0) + e * ROWS).astype(F32)
    m0 = jnp.where(key0 == want, 1.0, 0.0)
    m1 = jnp.where(key1 == want, 1.0, 0.0)
    other = jnp.sum(m0 * id1 + m1 * id0, axis=1, keepdims=True)
    first = jnp.sum(m0, axis=1, keepdims=True)
    misc = stacked(w_ref, 0)
    sub = lax.broadcasted_iota(jnp.int32, (8, 128), 0)
    take = (lanes(8) == L_GAIN + sub) & (sub < 3)
    gain = lax.dot_general(
        jnp.where(take, 1.0, 0.0).astype(BF), misc, NT, preferred_element_type=F32
    )
    scaled = res * jnp.sum(gain, axis=0, keepdims=True)
    sq = jnp.sum(res * res, axis=1, keepdims=True)
    high = scaled.astype(BF)
    low = (scaled - high.astype(F32)).astype(BF)
    logits = jnp.dot(high, misc, preferred_element_type=F32) + jnp.dot(
        low, misc, preferred_element_type=F32
    )
    lane = lanes(ROWS)
    stats = jnp.where((lane >= L_ROUTER) & (lane < L_ROUTER + 8), logits, 0.0)
    stats = jnp.where(lane == L_SQ, sq, stats)
    stats_high = stats.astype(BF).astype(F32)
    x_ref[:, 0:WIDE] = high
    x_ref[:, WIDE:] = (stats_high + pltpu.roll(stats - stats_high, 64, 1)).astype(BF)
    side_ref[...] = jnp.broadcast_to(other, (ROWS, 128))
    res_ref[...] = jnp.where(first > 0.5, res, 0.0)


def norm_body(s_ref, g_ref, side_ref, o_ref):
    e = s_ref[1]
    stats = g_ref[0, :, WIDE:].astype(F32)
    for z in range(1, NZ):
        stats += g_ref[z, :, WIDE:].astype(F32)
    stats = stats + pltpu.roll(stats, 64, 1)
    inverse = lax.rsqrt(stats[:, L_SQ : L_SQ + 1] / D + EPS)
    lane = lanes(ROWS)
    mine = jnp.sum(jnp.where(lane == L_ROUTER + e, stats, 0.0), axis=1, keepdims=True)
    rival = jnp.where(lane.astype(F32) == side_ref[...] + float(L_ROUTER), stats, 0.0)
    rival = jnp.sum(rival, axis=1, keepdims=True)
    gate = 1.0 / (1.0 + jnp.exp((rival - mine) * inverse))
    gate_high = gate.astype(BF).astype(F32)
    gates = jnp.where(lane == 0, gate_high, jnp.where(lane == 1, gate - gate_high, 0.0))
    gates = gates.astype(BF)
    for z in range(NZ):
        normed = (g_ref[z, :, 0:WIDE].astype(F32) * inverse).astype(BF)
        for n in range(NY):
            o_ref[n, :, z * WIDE : (z + 1) * WIDE] = normed
    for n in range(NY):
        o_ref[n, :, D:] = gates


def lift_body(x_ref, wg_ref, wu_ref, o_ref):
    gate = jnp.zeros((NY * ROWS, 128), F32)
    lift = jnp.zeros((NY * ROWS, 128), F32)
    for z in range(NZ):
        x = x_ref[:, z * WIDE : (z + 1) * WIDE]
        wg = jnp.concatenate([wg_ref[n, z] for n in range(NY)], axis=0)
        wu = jnp.concatenate([wu_ref[n, z] for n in range(NY)], axis=0)
        gate += jnp.dot(x, wg, preferred_element_type=F32)
        lift += jnp.dot(x, wu, preferred_element_type=F32)
    o_ref[...] = (gate / (1.0 + jnp.exp(-gate)) * lift).astype(BF)


def down_body(s_ref, h_ref, w_ref, gates_ref, res_ref, o_ref, sum_ref):
    y = s_ref[0]
    gates = gates_ref[...].astype(F32)
    gate = gates[:, 0:1] + gates[:, 1:2]
    mine = pl.ds(pl.multiple_of(y * ROWS, 8), ROWS)
    sums = jnp.zeros((NY * ROWS, WIDE), F32)
    for z in range(0, NZ, 4):
        h = jnp.concatenate([h_ref[z + i] for i in range(4)], axis=1)
        w = jnp.concatenate(
            [w_ref[n, :, z * 128 : (z + 4) * 128] for n in range(NY)], axis=0
        )
        sums += lax.dot_general(h, w, NT, preferred_element_type=F32)
    sum_ref[...] = gate * sums
    sum_ref[mine, :] += res_ref[...]
    total = sum_ref[...]
    for n in range(NY):
        for i in range(NE):
            piece = total[i * CAP : (i + 1) * CAP, n * FEAT : (n + 1) * FEAT]
            o_ref[n, i] = piece.astype(BF)


def swap(x, axis):
    return lax.all_to_all(x, axis, split_axis=0, concat_axis=0, tiled=True)


def shape(*dims, dtype=BF):
    return jax.ShapeDtypeStruct(dims, dtype)


def per_device(
    x_resid,
    queries,
    keys,
    values,
    pattern,
    global_blocks,
    out_weight,
    norm_gain,
    router,
    expert_ids,
    expert_slots,
    w_gate,
    w_up,
    w_down,
):
    y, z, e = lax.axis_index("y"), lax.axis_index("z"), lax.axis_index("exp")
    place = jnp.stack([y, e]).astype(jnp.int32)
    listed = jnp.concatenate([pattern[y], global_blocks, z[None].astype(jnp.int32)])

    pairs = jnp.concatenate([expert_ids.T, expert_slots.T], axis=0).astype(BF)
    blank = jnp.zeros_like(pairs)
    pairs = jnp.where(
        (e & 1) == 0,
        jnp.concatenate([pairs, blank], axis=1),
        jnp.concatenate([blank, pairs], axis=1),
    )
    pairs = jnp.pad(pairs, ((0, 12), (0, 0)))

    inputs = (keys, values, out_weight.T, x_resid, router.T, norm_gain[None])
    packed = call(
        pack_body, shape(NY, R_ALL, 128), [part(*a.shape) for a in inputs], mib=56
    )(*inputs)
    column = swap(packed, "y")
    block_queries = lax.all_gather(queries, "z", axis=0, tiled=True)

    partial = call(
        attend_body,
        shape(TOKB, (GROUP + 1) * HD),
        [VM] * 2,
        scratch=[pltpu.VMEM((GROUP * TOKB, 128), F32)] * 3,
        prefetch=1,
    )(listed, column, block_queries)
    partial, down = lax.optimization_barrier((partial, w_down[0].T))
    down = down.reshape(FEAT, NY, NZ * 128).swapaxes(0, 1)
    partial = swap(partial.reshape(NZ, TOKB // NZ, (GROUP + 1) * HD), "z")
    attention = call(merge_body, shape(NZ, TOKB // NZ, GROUP * HD), [VM])(partial)
    attention = swap(attention, "z").reshape(TOKB, GROUP * HD)
    ids = []
    for flip in range(2):
        route = [
            ((to_e >> 1) * NE + 2 * to_y + ((to_e & 1) ^ flip), to_y * NE + to_e)
            for to_y in range(NY)
            for to_e in range(NE)
        ]
        ids.append(lax.ppermute(pairs, ("y", "exp"), route))
    attention, *ids = lax.optimization_barrier((attention, *ids))
    ids = jnp.stack(ids)
    products = call(
        project_body,
        shape(NE * ROWS, WIDE),
        [VM, VM, VM],
        prefetch=1,
    )(place, attention, column, ids)
    products = swap(products.reshape(NE, ROWS, WIDE), "exp")
    rows, residual, side = call(
        pick_body,
        (
            shape(ROWS, WIDE + STATS),
            shape(ROWS, WIDE, dtype=F32),
            shape(ROWS, 128, dtype=F32),
        ),
        [VM, VM, VM],
        prefetch=1,
    )(place, products, column, ids)
    rows, down = lax.optimization_barrier((rows, down))
    down_column = swap(down, "y")
    gathered = lax.all_gather(rows, "z", axis=0)
    gathered, down_column = lax.optimization_barrier((gathered, down_column))
    normed = call(norm_body, shape(NY, ROWS, D + 128), [VM, VM], prefetch=1)(
        place, gathered, side
    )
    normed = swap(normed, "y").reshape(NY * ROWS, D + 128)

    hidden = call(lift_body, shape(NY * ROWS, 128), [VM] * 3)(
        normed, w_gate.reshape(NY, NZ, FEAT, 128), w_up.reshape(NY, NZ, FEAT, 128)
    )
    hidden = lax.all_gather(hidden, "z", axis=0)
    out = call(
        down_body,
        shape(NY, NE, CAP, FEAT),
        [
            VM,
            VM,
            part(NY * ROWS, 128, at=(0, D // 128)),
            VM,
        ],
        scratch=[pltpu.VMEM((NY * ROWS, WIDE), F32)],
        prefetch=1,
    )(place, hidden, down_column, normed, residual)
    back = swap(out.reshape(NY * NE, CAP, FEAT), ("y", "exp")).reshape(NY * NE * CAP, FEAT)
    flat = expert_ids * CAP + expert_slots
    at = jnp.arange(NY * NE * CAP, dtype=jnp.int32)[None, :] % (NE * CAP)
    both = ((flat[:, :1] == at) | (flat[:, 1:] == at)).astype(BF)
    return jnp.dot(both, back, preferred_element_type=F32).astype(BF)


def solution(mesh):
    inner = Mesh(mesh.devices.reshape(NY, NZ, NE), ("y", "z", "exp"))
    ctx = ("y", "z")
    in_specs = (
        P("exp", ctx),
        P(ctx, "exp"),
        P(ctx, "exp"),
        P(ctx, "exp"),
        P(),
        P(),
        P("exp", ctx),
        P(ctx),
        P(ctx, None),
        P("exp", None),
        P("exp", None),
        P("exp", None, ctx),
        P("exp", None, ctx),
        P("exp", None, ctx),
    )
    return jax.shard_map(
        per_device, mesh=inner, in_specs=in_specs, out_specs=P("exp", ctx), check_vma=False
    )
```

```python
import jax
import jax.numpy as jnp
from jax import lax
from jax.experimental import pallas as pl
from jax.experimental.pallas import tpu as pltpu
from jax.sharding import Mesh, PartitionSpec as P

D = 6144
HD = 128
BLK = 128
CAP = 20
NY, NZ, NE = 4, 16, 8
GROUP = 6
NSEL = 8
FEAT = 96
WIDE = NY * FEAT
TOKB = 128
ROWS = 2 * CAP
FIRST = -1e4
EPS = 1e-05
STATS = 128
R_W = FEAT
R_K = R_W + GROUP * FEAT
R_V = R_K + 4 * BLK
R_ALL = R_V + 4 * BLK
L_ROUTER, L_SQ, L_GAIN = 64, 72, 72
BF, F32 = jnp.bfloat16, jnp.float32
NT = (((1,), (1,)), ((), ()))


def call(body, out_shape, specs, scratch=(), prefetch=0, mib=40):
    params = pltpu.CompilerParams(vmem_limit_bytes=mib * 1024 * 1024)
    outs = jax.tree.map(lambda _: pl.BlockSpec(memory_space=pltpu.VMEM), out_shape)
    grid = pltpu.PrefetchScalarGridSpec(
        num_scalar_prefetch=prefetch,
        grid=(1,),
        in_specs=specs,
        out_specs=outs,
        scratch_shapes=list(scratch),
    )
    return pl.pallas_call(body, out_shape=out_shape, grid_spec=grid, compiler_params=params)


VM = pl.BlockSpec(memory_space=pltpu.VMEM)


def part(*block, at=None):
    at = (0,) * len(block) if at is None else at
    return pl.BlockSpec(block, lambda i, *s: at)


def lanes(rows, width=128):
    return lax.broadcasted_iota(jnp.int32, (rows, width), 1)


def pack_body(k_ref, v_ref, w_ref, x_ref, r_ref, g_ref, o_ref):
    gain = g_ref[...]
    hi = gain.astype(BF).astype(F32)
    mid = (gain - hi).astype(BF).astype(F32)
    lo = gain - hi - mid
    sub = lax.broadcasted_iota(jnp.int32, (8, FEAT), 0)
    gains = jnp.where(sub == 0, hi, jnp.where(sub == 1, mid, jnp.where(sub == 2, lo, 0.0)))
    blank = jnp.zeros((48, FEAT), F32)
    rows = jnp.concatenate([x_ref[...].astype(F32), r_ref[...].astype(F32), gains, blank], axis=0)
    eye = lax.broadcasted_iota(jnp.int32, (FEAT, FEAT), 0) == lanes(FEAT, FEAT)
    misc = lax.dot_general(
        jnp.where(eye, 1.0, 0.0).astype(BF), rows.astype(BF), NT, preferred_element_type=F32
    ).astype(BF)
    for y in range(NY):
        o_ref[y, 0:FEAT, :] = misc
        for g in range(GROUP):
            o_ref[y, R_W + g * FEAT : R_W + (g + 1) * FEAT, :] = w_ref[:, g * 128 : (g + 1) * 128]
        o_ref[y, R_K : R_K + 512, :] = k_ref[...]
        o_ref[y, R_V : R_V + 512, :] = v_ref[...]


def stacked(ref, start):
    return jnp.concatenate([ref[n, start : start + FEAT, :] for n in range(NY)], axis=0)


def attend_body(s_ref, kv_ref, q_ref, o_ref, acc_ref, m_ref, l_ref):
    acc_ref[...] = jnp.zeros_like(acc_ref)
    l_ref[...] = jnp.zeros_like(l_ref)
    m_ref[...] = jnp.full(m_ref.shape, FIRST, F32)
    here = s_ref[NSEL]
    for i in range(NSEL):
        block = s_ref[i]
        owner = block >> 2

        @pl.when((owner & (NZ - 1)) == here)
        def _():
            row = owner >> 4
            start = pl.multiple_of((block & 3) * BLK, BLK)
            keys = kv_ref[row, pl.ds(R_K + start, BLK), :]
            values = kv_ref[row, pl.ds(R_V + start, BLK), :]
            query = jnp.concatenate(
                [q_ref[:, g * HD : (g + 1) * HD] for g in range(GROUP)], axis=0
            )
            s = lax.dot_general(query, keys, NT, preferred_element_type=F32) * HD ** (-0.5)
            old = m_ref[...]
            new = jnp.maximum(old, jnp.max(s, axis=1, keepdims=True))
            p = jnp.exp(s - new).astype(BF)
            keep = jnp.exp(old - new)
            l_ref[...] = l_ref[...] * keep + jnp.sum(p.astype(F32), axis=1, keepdims=True)
            acc_ref[...] = acc_ref[...] * keep + jnp.dot(p, values, preferred_element_type=F32)
            m_ref[...] = new

    lane = lanes(TOKB)
    stats = jnp.zeros((TOKB, 128), F32)
    for g in range(GROUP):
        rows = slice(g * TOKB, (g + 1) * TOKB)
        m, l = m_ref[rows, :], l_ref[rows, :]
        o_ref[:, g * HD : (g + 1) * HD] = (acc_ref[rows, :] / jnp.where(l > 0, l, 1.0)).astype(BF)
        near = m.astype(BF).astype(F32)
        total = l * jnp.exp(m - near)
        high = total.astype(BF).astype(F32)
        stats = jnp.where(lane == g, near, stats)
        stats = jnp.where(lane == 8 + g, high, stats)
        stats = jnp.where(lane == 16 + g, total - high, stats)
    o_ref[:, GROUP * HD :] = stats.astype(BF)


def merge_body(r_ref, o_ref):
    got = r_ref[...].astype(F32)
    stats = got[:, :, GROUP * HD :]
    for g in range(GROUP):
        m = stats[:, :, g : g + 1]
        l = stats[:, :, 8 + g : 9 + g] + stats[:, :, 16 + g : 17 + g]
        weight = l * jnp.exp(m - jnp.max(m, axis=0, keepdims=True))
        top = jnp.sum(weight * got[:, :, g * HD : (g + 1) * HD], axis=0)
        out = (top / jnp.sum(weight, axis=0)).astype(BF)
        o_ref[:, :, g * HD : (g + 1) * HD] = jnp.broadcast_to(out[None], (NZ,) + out.shape)


def slot_keys(ids_ref):
    ids = ids_ref[...].astype(F32)
    id0, id1, slot0, slot1 = (ids[i : i + 1, :] for i in range(4))
    base = jnp.where(lanes(1) >= 64, float(CAP), 0.0)
    return id0 * ROWS + slot0 + base, id1 * ROWS + slot1 + base, id0, id1


def project_body(s_ref, a_ref, w_ref, ids_ref, o_ref):
    y, e = s_ref[0], s_ref[1]
    total = jnp.zeros((TOKB, WIDE), F32)
    for g in range(GROUP):
        total += lax.dot_general(
            a_ref[:, g * 128 : (g + 1) * 128],
            stacked(w_ref, R_W + g * FEAT),
            NT,
            preferred_element_type=F32,
        )
    row = lax.broadcasted_iota(jnp.int32, (TOKB, 128), 0)
    mine = (row == lanes(TOKB) + (e & 1) * 64) & (lanes(TOKB) < 64) & ((e >> 1) == y)
    total += lax.dot_general(
        jnp.where(mine, 1.0, 0.0).astype(BF),
        stacked(w_ref, 0),
        NT,
        preferred_element_type=F32,
    )
    key0, key1, _, _ = slot_keys(ids_ref)
    want = lax.broadcasted_iota(jnp.int32, (NE * ROWS, 128), 0).astype(F32)
    choose = jnp.where((key0 == want) | (key1 == want), 1.0, 0.0).astype(BF)
    o_ref[...] = jnp.dot(choose, total.astype(BF), preferred_element_type=F32).astype(BF)


def pick_body(s_ref, r_ref, w_ref, ids_ref, x_ref, res_ref, side_ref):
    e = s_ref[1]
    res = r_ref[0].astype(F32)
    for n in range(1, NE):
        res += r_ref[n].astype(F32)
    key0, key1, id0, id1 = slot_keys(ids_ref)
    want = (lax.broadcasted_iota(jnp.int32, (ROWS, 128), 0) + e * ROWS).astype(F32)
    m0 = jnp.where(key0 == want, 1.0, 0.0)
    m1 = jnp.where(key1 == want, 1.0, 0.0)
    other = jnp.sum(m0 * id1 + m1 * id0, axis=1, keepdims=True)
    first = jnp.sum(m0, axis=1, keepdims=True)
    misc = stacked(w_ref, 0)
    sub = lax.broadcasted_iota(jnp.int32, (8, 128), 0)
    take = (lanes(8) == L_GAIN + sub) & (sub < 3)
    gain = lax.dot_general(
        jnp.where(take, 1.0, 0.0).astype(BF), misc, NT, preferred_element_type=F32
    )
    scaled = res * jnp.sum(gain, axis=0, keepdims=True)
    sq = jnp.sum(res * res, axis=1, keepdims=True)
    high = scaled.astype(BF)
    low = (scaled - high.astype(F32)).astype(BF)
    logits = jnp.dot(high, misc, preferred_element_type=F32) + jnp.dot(
        low, misc, preferred_element_type=F32
    )
    lane = lanes(ROWS)
    stats = jnp.where((lane >= L_ROUTER) & (lane < L_ROUTER + 8), logits, 0.0)
    stats = jnp.where(lane == L_SQ, sq, stats)
    stats_high = stats.astype(BF).astype(F32)
    x_ref[:, 0:WIDE] = high
    x_ref[:, WIDE:] = (stats_high + pltpu.roll(stats - stats_high, 64, 1)).astype(BF)
    side_ref[...] = jnp.broadcast_to(other, (ROWS, 128))
    res_ref[...] = jnp.where(first > 0.5, res, 0.0)


def norm_body(s_ref, g_ref, side_ref, o_ref):
    e = s_ref[1]
    stats = g_ref[0, :, WIDE:].astype(F32)
    for z in range(1, NZ):
        stats += g_ref[z, :, WIDE:].astype(F32)
    stats = stats + pltpu.roll(stats, 64, 1)
    inverse = lax.rsqrt(stats[:, L_SQ : L_SQ + 1] / D + EPS)
    lane = lanes(ROWS)
    mine = jnp.sum(jnp.where(lane == L_ROUTER + e, stats, 0.0), axis=1, keepdims=True)
    rival = jnp.where(lane.astype(F32) == side_ref[...] + float(L_ROUTER), stats, 0.0)
    rival = jnp.sum(rival, axis=1, keepdims=True)
    gate = 1.0 / (1.0 + jnp.exp((rival - mine) * inverse))
    gate_high = gate.astype(BF).astype(F32)
    gates = jnp.where(lane == 0, gate_high, jnp.where(lane == 1, gate - gate_high, 0.0))
    gates = gates.astype(BF)
    for z in range(NZ):
        normed = (g_ref[z, :, 0:WIDE].astype(F32) * inverse).astype(BF)
        for n in range(NY):
            o_ref[n, :, z * WIDE : (z + 1) * WIDE] = normed
    for n in range(NY):
        o_ref[n, :, D:] = gates


def lift_body(x_ref, wg_ref, wu_ref, o_ref):
    gate = jnp.zeros((NY * ROWS, 128), F32)
    lift = jnp.zeros((NY * ROWS, 128), F32)
    for z in range(NZ):
        x = x_ref[:, z * WIDE : (z + 1) * WIDE]
        wg = jnp.concatenate([wg_ref[n, z] for n in range(NY)], axis=0)
        wu = jnp.concatenate([wu_ref[n, z] for n in range(NY)], axis=0)
        gate += jnp.dot(x, wg, preferred_element_type=F32)
        lift += jnp.dot(x, wu, preferred_element_type=F32)
    o_ref[...] = (gate / (1.0 + jnp.exp(-gate)) * lift).astype(BF)


def down_body(s_ref, h_ref, w_ref, gates_ref, res_ref, o_ref, sum_ref):
    y = s_ref[0]
    gates = gates_ref[...].astype(F32)
    gate = gates[:, 0:1] + gates[:, 1:2]
    mine = pl.ds(pl.multiple_of(y * ROWS, 8), ROWS)
    sums = jnp.zeros((NY * ROWS, WIDE), F32)
    for z in range(0, NZ, 4):
        h = jnp.concatenate([h_ref[z + i] for i in range(4)], axis=1)
        w = jnp.concatenate(
            [w_ref[n, :, z * 128 : (z + 4) * 128] for n in range(NY)], axis=0
        )
        sums += lax.dot_general(h, w, NT, preferred_element_type=F32)
    sum_ref[...] = gate * sums
    sum_ref[mine, :] += res_ref[...]
    total = sum_ref[...]
    for n in range(NY):
        for i in range(NE):
            piece = total[i * CAP : (i + 1) * CAP, n * FEAT : (n + 1) * FEAT]
            o_ref[n, i] = piece.astype(BF)


def swap(x, axis):
    return lax.all_to_all(x, axis, split_axis=0, concat_axis=0, tiled=True)


def shape(*dims, dtype=BF):
    return jax.ShapeDtypeStruct(dims, dtype)


def per_device(
    x_resid,
    queries,
    keys,
    values,
    pattern,
    global_blocks,
    out_weight,
    norm_gain,
    router,
    expert_ids,
    expert_slots,
    w_gate,
    w_up,
    w_down,
):
    y, z, e = lax.axis_index("y"), lax.axis_index("z"), lax.axis_index("exp")
    place = jnp.stack([y, e]).astype(jnp.int32)
    listed = jnp.concatenate([pattern[y], global_blocks, z[None].astype(jnp.int32)])

    pairs = jnp.concatenate([expert_ids.T, expert_slots.T], axis=0).astype(BF)
    blank = jnp.zeros_like(pairs)
    pairs = jnp.where(
        (e & 1) == 0,
        jnp.concatenate([pairs, blank], axis=1),
        jnp.concatenate([blank, pairs], axis=1),
    )
    pairs = jnp.pad(pairs, ((0, 12), (0, 0)))

    inputs = (keys, values, out_weight.T, x_resid, router.T, norm_gain[None])
    packed = call(
        pack_body, shape(NY, R_ALL, 128), [part(*a.shape) for a in inputs], mib=56
    )(*inputs)
    column = swap(packed, "y")
    block_queries = lax.all_gather(queries, "z", axis=0, tiled=True)

    partial = call(
        attend_body,
        shape(TOKB, (GROUP + 1) * HD),
        [VM] * 2,
        scratch=[pltpu.VMEM((GROUP * TOKB, 128), F32)] * 3,
        prefetch=1,
    )(listed, column, block_queries)
    partial, down = lax.optimization_barrier((partial, w_down[0].T))
    down = down.reshape(FEAT, NY, NZ * 128).swapaxes(0, 1)
    twins = pairs + lax.ppermute(pairs, "exp", [(i, i ^ 1) for i in range(NE)])
    partial = swap(partial.reshape(NZ, TOKB // NZ, (GROUP + 1) * HD), "z")
    partial, twins = lax.optimization_barrier((partial, twins))
    attention = call(merge_body, shape(NZ, TOKB // NZ, GROUP * HD), [VM])(partial)
    attention = swap(attention, "z").reshape(TOKB, GROUP * HD)
    route = [
        ((to_e >> 1) * NE + 2 * to_y + (to_e & 1), to_y * NE + to_e)
        for to_y in range(NY)
        for to_e in range(NE)
    ]
    ids = lax.ppermute(twins, ("y", "exp"), route)
    attention, ids = lax.optimization_barrier((attention, ids))

    products = call(
        project_body,
        shape(NE * ROWS, WIDE),
        [VM, VM, VM],
        prefetch=1,
    )(place, attention, column, ids)
    products = swap(products.reshape(NE, ROWS, WIDE), "exp")
    rows, residual, side = call(
        pick_body,
        (
            shape(ROWS, WIDE + STATS),
            shape(ROWS, WIDE, dtype=F32),
            shape(ROWS, 128, dtype=F32),
        ),
        [VM, VM, VM],
        prefetch=1,
    )(place, products, column, ids)
    rows, down = lax.optimization_barrier((rows, down))
    down_column = swap(down, "y")
    gathered = lax.all_gather(rows, "z", axis=0)
    gathered, down_column = lax.optimization_barrier((gathered, down_column))
    normed = call(norm_body, shape(NY, ROWS, D + 128), [VM, VM], prefetch=1)(
        place, gathered, side
    )
    normed = swap(normed, "y").reshape(NY * ROWS, D + 128)

    hidden = call(lift_body, shape(NY * ROWS, 128), [VM] * 3)(
        normed, w_gate.reshape(NY, NZ, FEAT, 128), w_up.reshape(NY, NZ, FEAT, 128)
    )
    hidden = lax.all_gather(hidden, "z", axis=0)
    out = call(
        down_body,
        shape(NY, NE, CAP, FEAT),
        [
            VM,
            VM,
            part(NY * ROWS, 128, at=(0, D // 128)),
            VM,
        ],
        scratch=[pltpu.VMEM((NY * ROWS, WIDE), F32)],
        prefetch=1,
    )(place, hidden, down_column, normed, residual)
    back = swap(out.reshape(NY * NE, CAP, FEAT), ("y", "exp")).reshape(NY * NE * CAP, FEAT)
    flat = expert_ids * CAP + expert_slots
    at = jnp.arange(NY * NE * CAP, dtype=jnp.int32)[None, :] % (NE * CAP)
    both = ((flat[:, :1] == at) | (flat[:, 1:] == at)).astype(BF)
    return jnp.dot(both, back, preferred_element_type=F32).astype(BF)


def solution(mesh):
    inner = Mesh(mesh.devices.reshape(NY, NZ, NE), ("y", "z", "exp"))
    ctx = ("y", "z")
    in_specs = (
        P("exp", ctx),
        P(ctx, "exp"),
        P(ctx, "exp"),
        P(ctx, "exp"),
        P(),
        P(),
        P("exp", ctx),
        P(ctx),
        P(ctx, None),
        P("exp", None),
        P("exp", None),
        P("exp", None, ctx),
        P("exp", None, ctx),
        P("exp", None, ctx),
    )
    return jax.shard_map(
        per_device, mesh=inner, in_specs=in_specs, out_specs=P("exp", ctx), check_vma=False
    )
```

```python
import jax
import jax.numpy as jnp
from jax import lax
from jax.experimental import pallas as pl
from jax.experimental.pallas import tpu as pltpu
from jax.sharding import Mesh, PartitionSpec as P

D = 6144
HD = 128
BLK = 128
CAP = 20
NY, NZ, NE = 4, 16, 8
GROUP = 6
NSEL = 8
FEAT = 96
WIDE = NY * FEAT
TOKB = 128
ROWS = 2 * CAP
FIRST = -1e4
EPS = 1e-05
STATS = 128
R_W = FEAT
R_K = R_W + GROUP * FEAT
R_V = R_K + 4 * BLK
R_ALL = R_V + 4 * BLK
L_ROUTER, L_SQ, L_GAIN = 64, 72, 72
BF, F32 = jnp.bfloat16, jnp.float32
NT = (((1,), (1,)), ((), ()))


def call(body, out_shape, specs, scratch=(), prefetch=0, mib=40):
    params = pltpu.CompilerParams(vmem_limit_bytes=mib * 1024 * 1024)
    outs = jax.tree.map(lambda _: pl.BlockSpec(memory_space=pltpu.VMEM), out_shape)
    grid = pltpu.PrefetchScalarGridSpec(
        num_scalar_prefetch=prefetch,
        grid=(1,),
        in_specs=specs,
        out_specs=outs,
        scratch_shapes=list(scratch),
    )
    return pl.pallas_call(body, out_shape=out_shape, grid_spec=grid, compiler_params=params)


VM = pl.BlockSpec(memory_space=pltpu.VMEM)


def part(*block, at=None):
    at = (0,) * len(block) if at is None else at
    return pl.BlockSpec(block, lambda i, *s: at)


def lanes(rows, width=128):
    return lax.broadcasted_iota(jnp.int32, (rows, width), 1)


def pack_body(k_ref, v_ref, w_ref, x_ref, r_ref, g_ref, o_ref):
    gain = g_ref[...]
    hi = gain.astype(BF).astype(F32)
    mid = (gain - hi).astype(BF).astype(F32)
    lo = gain - hi - mid
    sub = lax.broadcasted_iota(jnp.int32, (8, FEAT), 0)
    gains = jnp.where(sub == 0, hi, jnp.where(sub == 1, mid, jnp.where(sub == 2, lo, 0.0)))
    blank = jnp.zeros((48, FEAT), F32)
    rows = jnp.concatenate([x_ref[...].astype(F32), r_ref[...].astype(F32), gains, blank], axis=0)
    eye = lax.broadcasted_iota(jnp.int32, (FEAT, FEAT), 0) == lanes(FEAT, FEAT)
    misc = lax.dot_general(
        jnp.where(eye, 1.0, 0.0).astype(BF), rows.astype(BF), NT, preferred_element_type=F32
    ).astype(BF)
    for y in range(NY):
        o_ref[y, 0:FEAT, :] = misc
        for g in range(GROUP):
            o_ref[y, R_W + g * FEAT : R_W + (g + 1) * FEAT, :] = w_ref[:, g * 128 : (g + 1) * 128]
        o_ref[y, R_K : R_K + 512, :] = k_ref[...]
        o_ref[y, R_V : R_V + 512, :] = v_ref[...]


def stacked(ref, start):
    return jnp.concatenate([ref[n, start : start + FEAT, :] for n in range(NY)], axis=0)


def attend_body(s_ref, kv_ref, q_ref, o_ref, acc_ref, m_ref, l_ref):
    acc_ref[...] = jnp.zeros_like(acc_ref)
    l_ref[...] = jnp.zeros_like(l_ref)
    m_ref[...] = jnp.full(m_ref.shape, FIRST, F32)
    here = s_ref[NSEL]
    for i in range(NSEL):
        block = s_ref[i]
        owner = block >> 2

        @pl.when((owner & (NZ - 1)) == here)
        def _():
            row = owner >> 4
            start = pl.multiple_of((block & 3) * BLK, BLK)
            keys = kv_ref[row, pl.ds(R_K + start, BLK), :]
            values = kv_ref[row, pl.ds(R_V + start, BLK), :]
            query = jnp.concatenate(
                [q_ref[:, g * HD : (g + 1) * HD] for g in range(GROUP)], axis=0
            )
            s = lax.dot_general(query, keys, NT, preferred_element_type=F32) * HD ** (-0.5)
            old = m_ref[...]
            new = jnp.maximum(old, jnp.max(s, axis=1, keepdims=True))
            p = jnp.exp(s - new).astype(BF)
            keep = jnp.exp(old - new)
            l_ref[...] = l_ref[...] * keep + jnp.sum(p.astype(F32), axis=1, keepdims=True)
            acc_ref[...] = acc_ref[...] * keep + jnp.dot(p, values, preferred_element_type=F32)
            m_ref[...] = new

    lane = lanes(TOKB)
    stats = jnp.zeros((TOKB, 128), F32)
    for g in range(GROUP):
        rows = slice(g * TOKB, (g + 1) * TOKB)
        m, l = m_ref[rows, :], l_ref[rows, :]
        o_ref[:, g * HD : (g + 1) * HD] = (acc_ref[rows, :] / jnp.where(l > 0, l, 1.0)).astype(BF)
        near = m.astype(BF).astype(F32)
        total = l * jnp.exp(m - near)
        high = total.astype(BF).astype(F32)
        stats = jnp.where(lane == g, near, stats)
        stats = jnp.where(lane == 8 + g, high, stats)
        stats = jnp.where(lane == 16 + g, total - high, stats)
    o_ref[:, GROUP * HD :] = stats.astype(BF)


def merge_body(r_ref, o_ref):
    got = r_ref[...].astype(F32)
    stats = got[:, :, GROUP * HD :]
    for g in range(GROUP):
        m = stats[:, :, g : g + 1]
        l = stats[:, :, 8 + g : 9 + g] + stats[:, :, 16 + g : 17 + g]
        weight = l * jnp.exp(m - jnp.max(m, axis=0, keepdims=True))
        top = jnp.sum(weight * got[:, :, g * HD : (g + 1) * HD], axis=0)
        out = (top / jnp.sum(weight, axis=0)).astype(BF)
        o_ref[:, :, g * HD : (g + 1) * HD] = jnp.broadcast_to(out[None], (NZ,) + out.shape)


def slot_keys(ids_ref):
    ids = ids_ref[...].astype(F32)
    id0, id1, slot0, slot1 = (ids[i : i + 1, :] for i in range(4))
    base = jnp.where(lanes(1) >= 64, float(CAP), 0.0)
    return id0 * ROWS + slot0 + base, id1 * ROWS + slot1 + base, id0, id1


def project_body(s_ref, a_ref, w_ref, ids_ref, o_ref):
    y, e = s_ref[0], s_ref[1]
    total = jnp.zeros((TOKB, WIDE), F32)
    for g in range(GROUP):
        total += lax.dot_general(
            a_ref[:, g * 128 : (g + 1) * 128],
            stacked(w_ref, R_W + g * FEAT),
            NT,
            preferred_element_type=F32,
        )
    row = lax.broadcasted_iota(jnp.int32, (TOKB, 128), 0)
    mine = (row == lanes(TOKB) + (e & 1) * 64) & (lanes(TOKB) < 64) & ((e >> 1) == y)
    total += lax.dot_general(
        jnp.where(mine, 1.0, 0.0).astype(BF),
        stacked(w_ref, 0),
        NT,
        preferred_element_type=F32,
    )
    key0, key1, _, _ = slot_keys(ids_ref)
    want = lax.broadcasted_iota(jnp.int32, (NE * ROWS, 128), 0).astype(F32)
    choose = jnp.where((key0 == want) | (key1 == want), 1.0, 0.0).astype(BF)
    o_ref[...] = jnp.dot(choose, total.astype(BF), preferred_element_type=F32).astype(BF)


def pick_body(s_ref, r_ref, w_ref, ids_ref, x_ref, res_ref, side_ref):
    e = s_ref[1]
    res = r_ref[0].astype(F32)
    for n in range(1, NE):
        res += r_ref[n].astype(F32)
    key0, key1, id0, id1 = slot_keys(ids_ref)
    want = (lax.broadcasted_iota(jnp.int32, (ROWS, 128), 0) + e * ROWS).astype(F32)
    m0 = jnp.where(key0 == want, 1.0, 0.0)
    m1 = jnp.where(key1 == want, 1.0, 0.0)
    other = jnp.sum(m0 * id1 + m1 * id0, axis=1, keepdims=True)
    first = jnp.sum(m0, axis=1, keepdims=True)
    misc = stacked(w_ref, 0)
    sub = lax.broadcasted_iota(jnp.int32, (8, 128), 0)
    take = (lanes(8) == L_GAIN + sub) & (sub < 3)
    gain = lax.dot_general(
        jnp.where(take, 1.0, 0.0).astype(BF), misc, NT, preferred_element_type=F32
    )
    scaled = res * jnp.sum(gain, axis=0, keepdims=True)
    sq = jnp.sum(res * res, axis=1, keepdims=True)
    high = scaled.astype(BF)
    low = (scaled - high.astype(F32)).astype(BF)
    logits = jnp.dot(high, misc, preferred_element_type=F32) + jnp.dot(
        low, misc, preferred_element_type=F32
    )
    lane = lanes(ROWS)
    stats = jnp.where((lane >= L_ROUTER) & (lane < L_ROUTER + 8), logits, 0.0)
    stats = jnp.where(lane == L_SQ, sq, stats)
    stats_high = stats.astype(BF).astype(F32)
    x_ref[:, 0:WIDE] = high
    x_ref[:, WIDE:] = (stats_high + pltpu.roll(stats - stats_high, 64, 1)).astype(BF)
    side_ref[...] = jnp.broadcast_to(other, (ROWS, 128))
    res_ref[...] = jnp.where(first > 0.5, res, 0.0)


def norm_body(s_ref, g_ref, side_ref, o_ref):
    e = s_ref[1]
    stats = g_ref[0, :, WIDE:].astype(F32)
    for z in range(1, NZ):
        stats += g_ref[z, :, WIDE:].astype(F32)
    stats = stats + pltpu.roll(stats, 64, 1)
    inverse = lax.rsqrt(stats[:, L_SQ : L_SQ + 1] / D + EPS)
    lane = lanes(ROWS)
    mine = jnp.sum(jnp.where(lane == L_ROUTER + e, stats, 0.0), axis=1, keepdims=True)
    rival = jnp.where(lane.astype(F32) == side_ref[...] + float(L_ROUTER), stats, 0.0)
    rival = jnp.sum(rival, axis=1, keepdims=True)
    gate = 1.0 / (1.0 + jnp.exp((rival - mine) * inverse))
    gate_high = gate.astype(BF).astype(F32)
    gates = jnp.where(lane == 0, gate_high, jnp.where(lane == 1, gate - gate_high, 0.0))
    gates = gates.astype(BF)
    for z in range(NZ):
        normed = (g_ref[z, :, 0:WIDE].astype(F32) * inverse).astype(BF)
        for n in range(NY):
            o_ref[n, :, z * WIDE : (z + 1) * WIDE] = normed
    for n in range(NY):
        o_ref[n, :, D:] = gates


def lift_body(x_ref, wg_ref, wu_ref, o_ref):
    gate = jnp.zeros((NY * ROWS, 128), F32)
    lift = jnp.zeros((NY * ROWS, 128), F32)
    for z in range(NZ):
        x = x_ref[:, z * WIDE : (z + 1) * WIDE]
        wg = jnp.concatenate([wg_ref[n, z] for n in range(NY)], axis=0)
        wu = jnp.concatenate([wu_ref[n, z] for n in range(NY)], axis=0)
        gate += jnp.dot(x, wg, preferred_element_type=F32)
        lift += jnp.dot(x, wu, preferred_element_type=F32)
    o_ref[...] = (gate / (1.0 + jnp.exp(-gate)) * lift).astype(BF)


def down_body(s_ref, h_ref, w_ref, gates_ref, res_ref, o_ref, sum_ref):
    y = s_ref[0]
    gates = gates_ref[...].astype(F32)
    gate = gates[:, 0:1] + gates[:, 1:2]
    mine = pl.ds(pl.multiple_of(y * ROWS, 8), ROWS)
    sums = jnp.zeros((NY * ROWS, WIDE), F32)
    for z in range(0, NZ, 4):
        h = jnp.concatenate([h_ref[z + i] for i in range(4)], axis=1)
        w = jnp.concatenate(
            [w_ref[n, :, z * 128 : (z + 4) * 128] for n in range(NY)], axis=0
        )
        sums += lax.dot_general(h, w, NT, preferred_element_type=F32)
    sum_ref[...] = gate * sums
    sum_ref[mine, :] += res_ref[...]
    total = sum_ref[...]
    for n in range(NY):
        for i in range(NE):
            piece = total[i * CAP : (i + 1) * CAP, n * FEAT : (n + 1) * FEAT]
            o_ref[n, i] = piece.astype(BF)


def swap(x, axis):
    return lax.all_to_all(x, axis, split_axis=0, concat_axis=0, tiled=True)


def shape(*dims, dtype=BF):
    return jax.ShapeDtypeStruct(dims, dtype)


def per_device(
    x_resid,
    queries,
    keys,
    values,
    pattern,
    global_blocks,
    out_weight,
    norm_gain,
    router,
    expert_ids,
    expert_slots,
    w_gate,
    w_up,
    w_down,
):
    y, z, e = lax.axis_index("y"), lax.axis_index("z"), lax.axis_index("exp")
    place = jnp.stack([y, e]).astype(jnp.int32)
    listed = jnp.concatenate([pattern[y], global_blocks, z[None].astype(jnp.int32)])

    pairs = jnp.concatenate([expert_ids.T, expert_slots.T], axis=0).astype(BF)
    blank = jnp.zeros_like(pairs)
    pairs = jnp.where(
        (e & 1) == 0,
        jnp.concatenate([pairs, blank], axis=1),
        jnp.concatenate([blank, pairs], axis=1),
    )
    pairs = jnp.pad(pairs, ((0, 12), (0, 0)))

    inputs = (keys, values, out_weight.T, x_resid, router.T, norm_gain[None])
    packed = call(
        pack_body, shape(NY, R_ALL, 128), [part(*a.shape) for a in inputs], mib=56
    )(*inputs)
    column = swap(packed, "y")
    block_queries = lax.all_gather(queries, "z", axis=0, tiled=True)

    partial = call(
        attend_body,
        shape(TOKB, (GROUP + 1) * HD),
        [VM] * 2,
        scratch=[pltpu.VMEM((GROUP * TOKB, 128), F32)] * 3,
        prefetch=1,
    )(listed, column, block_queries)
    partial, down = lax.optimization_barrier((partial, w_down[0].T))
    down = down.reshape(FEAT, NY, NZ * 128).swapaxes(0, 1)
    twins = pairs + lax.ppermute(pairs, "exp", [(i, i ^ 1) for i in range(NE)])
    partial = swap(partial.reshape(NZ, TOKB // NZ, (GROUP + 1) * HD), "z")
    partial, twins, down = lax.optimization_barrier((partial, twins, down))
    attention = call(merge_body, shape(NZ, TOKB // NZ, GROUP * HD), [VM])(partial)
    attention = swap(attention, "z").reshape(TOKB, GROUP * HD)
    route = [
        ((to_e >> 1) * NE + 2 * to_y + (to_e & 1), to_y * NE + to_e)
        for to_y in range(NY)
        for to_e in range(NE)
    ]
    ids = lax.ppermute(twins, ("y", "exp"), route)
    attention, ids = lax.optimization_barrier((attention, ids))

    products = call(
        project_body,
        shape(NE * ROWS, WIDE),
        [VM, VM, VM],
        prefetch=1,
    )(place, attention, column, ids)
    products = swap(products.reshape(NE, ROWS, WIDE), "exp")
    rows, residual, side = call(
        pick_body,
        (
            shape(ROWS, WIDE + STATS),
            shape(ROWS, WIDE, dtype=F32),
            shape(ROWS, 128, dtype=F32),
        ),
        [VM, VM, VM],
        prefetch=1,
    )(place, products, column, ids)
    rows, down = lax.optimization_barrier((rows, down))
    down_column = swap(down, "y")
    gathered = lax.all_gather(rows, "z", axis=0)
    gathered, down_column = lax.optimization_barrier((gathered, down_column))
    normed = call(norm_body, shape(NY, ROWS, D + 128), [VM, VM], prefetch=1)(
        place, gathered, side
    )
    normed = swap(normed, "y").reshape(NY * ROWS, D + 128)

    hidden = call(lift_body, shape(NY * ROWS, 128), [VM] * 3)(
        normed, w_gate.reshape(NY, NZ, FEAT, 128), w_up.reshape(NY, NZ, FEAT, 128)
    )
    hidden = lax.all_gather(hidden, "z", axis=0)
    out = call(
        down_body,
        shape(NY, NE, CAP, FEAT),
        [
            VM,
            VM,
            part(NY * ROWS, 128, at=(0, D // 128)),
            VM,
        ],
        scratch=[pltpu.VMEM((NY * ROWS, WIDE), F32)],
        prefetch=1,
    )(place, hidden, down_column, normed, residual)
    back = swap(out.reshape(NY * NE, CAP, FEAT), ("y", "exp")).reshape(NY * NE * CAP, FEAT)
    flat = expert_ids * CAP + expert_slots
    at = jnp.arange(NY * NE * CAP, dtype=jnp.int32)[None, :] % (NE * CAP)
    both = ((flat[:, :1] == at) | (flat[:, 1:] == at)).astype(BF)
    return jnp.dot(both, back, preferred_element_type=F32).astype(BF)


def solution(mesh):
    inner = Mesh(mesh.devices.reshape(NY, NZ, NE), ("y", "z", "exp"))
    ctx = ("y", "z")
    in_specs = (
        P("exp", ctx),
        P(ctx, "exp"),
        P(ctx, "exp"),
        P(ctx, "exp"),
        P(),
        P(),
        P("exp", ctx),
        P(ctx),
        P(ctx, None),
        P("exp", None),
        P("exp", None),
        P("exp", None, ctx),
        P("exp", None, ctx),
        P("exp", None, ctx),
    )
    return jax.shard_map(
        per_device, mesh=inner, in_specs=in_specs, out_specs=P("exp", ctx), check_vma=False
    )
```
